512 devices in a mesh: ctx: 128 (over z, y, core), head: 4 (over x).
Axes of the slice: x: 4, y: 4, z: 16, core: 2. Of those that a mesh axis runs over, the one named last changes fastest.
Arguments:
- queries: bfloat16 [32768, 12288], P(('ctx', 'head')), may hold values from -96 to 96
- key_rows: bfloat16 [32768, 768], P(('ctx', 'head')), may hold values from -8 to 8
- values: bfloat16 [32768, 512], P(('ctx', 'head')), may hold values from -6 to 6
- gate_logits: bfloat16 [32768, 128], P(('ctx', 'head')), may hold values from -6 to 6
- key_mix: bfloat16 [4, 32, 192], replicated, may hold values from -1 to 1
- key_proj: bfloat16 [4, 192, 192], replicated, may hold values from -1 to 1
- value_mix: bfloat16 [4, 32, 128], replicated, may hold values from -1 to 1
- value_proj: bfloat16 [4, 128, 128], replicated, may hold values from -0.5 to 0.5
Outputs:
- mixture: bfloat16 [32768, 8192], P(('ctx', 'head'))
The draws below stay inside these ranges and needn't reach their ends.
All inputs are finite; a program needn't handle non-finite values.
Results may differ from the reference program's by a relative error of at most 0.012.
Values may be sent and summed in bfloat16 or wider, within the bound.
A program may use at most 64 MiB of HBM per device.

```python
import math
import jax
import jax.numpy as jnp
from jax import lax

QHEADS = 64
GROUPS = 4
KDIM = 192
VDIM = 128
BLOCK = 32
STRIDE = 16
WINDOW = 512
TOKENS = 32768
NBLOCKS = 2048


def base_draws(key):
    key_first = jax.random.fold_in(key, 101)
    key_second = jax.random.fold_in(key, 102)
    key_third = jax.random.fold_in(key, 103)
    rows_raw = jax.random.normal(key_first, (TOKENS, GROUPS, KDIM), jnp.float32)
    mixer = jax.random.normal(key_second, (GROUPS, BLOCK, KDIM), jnp.float32) / math.sqrt(BLOCK)
    projection = jax.random.normal(key_third, (GROUPS, KDIM, KDIM), jnp.float32) / math.sqrt(KDIM)
    rows_out = jnp.clip(rows_raw, -8.0, 8.0).astype(jnp.bfloat16)
    mixer = jnp.clip(mixer, -1.0, 1.0).astype(jnp.bfloat16)
    projection = jnp.clip(projection, -1.0, 1.0).astype(jnp.bfloat16)
    return (rows_out, mixer, projection)


def draw_queries(key, part):
    key_base = jax.random.fold_in(key, 201)
    drawn = jax.random.normal(key_base, (TOKENS, QHEADS, KDIM), jnp.float32) * 2.0
    drawn = jnp.clip(drawn, -8.0, 8.0)
    return drawn.reshape(TOKENS, QHEADS * KDIM).astype(jnp.bfloat16)


def draw_key_rows(key, part):
    rows_key, mixer, projection = base_draws(key)
    return rows_key.reshape(TOKENS, GROUPS * KDIM)


def draw_key_mix(key, part):
    rows_key, mixer, projection = base_draws(key)
    return mixer


def draw_key_proj(key, part):
    rows_key, mixer, projection = base_draws(key)
    return projection


def block_levels(own_key, extent, shards, least, largest):
    level, own = 1.0, jax.random.fold_in(own_key, 6)
    for axis_at, parts in shards:
        steps = jnp.exp(jax.random.uniform(jax.random.fold_in(own, axis_at), (parts,), jnp.float32, least / len(shards), largest / len(shards)))
        level = level * jnp.repeat(steps, extent[axis_at] // parts).reshape([-1 if axis == axis_at else 1 for axis in range(len(extent))])
    return level


def gaussian(own_key, extent, scale, reach, shards=(), kind=jnp.bfloat16):
    values = scale * jax.random.normal(own_key, extent, jnp.float32)
    if shards:
        values = values * block_levels(own_key, extent, shards, -0.22, 0.18)
    return jnp.clip(values, -reach, reach).astype(kind)


def setup_inputs(seed: int = 0) -> dict:
    keys = jax.random.split(jax.random.key(seed), 9)
    return {
        "queries": draw_queries(jax.random.fold_in(keys[8], 71), 0),
        "key_rows": draw_key_rows(jax.random.fold_in(keys[8], 71), 0),
        "values": gaussian(keys[2], (TOKENS, GROUPS * VDIM), 1.0, 6.0, ((0, 512),)),
        "gate_logits": gaussian(keys[3], (TOKENS, 2 * QHEADS), 1.5, 6.0, ((0, 512),)),
        "key_mix": draw_key_mix(jax.random.fold_in(keys[8], 71), 0),
        "key_proj": draw_key_proj(jax.random.fold_in(keys[8], 71), 0),
        "value_mix": gaussian(keys[6], (GROUPS, BLOCK, VDIM), 0.177, 1.0),
        "value_proj": gaussian(keys[7], (GROUPS, VDIM, VDIM), VDIM ** -0.5, 0.5),
    }


def compress_rows(rows, mixer, projection):
    block_count = rows.shape[0] // STRIDE
    zero_rows = jnp.zeros((STRIDE, rows.shape[1], rows.shape[2]), jnp.float32)
    padded = jnp.concatenate([rows.astype(jnp.float32), zero_rows], 0)
    halves = padded.reshape(block_count + 1, STRIDE, rows.shape[1], rows.shape[2])
    weights = mixer.astype(jnp.float32)
    pooled = jnp.einsum('bjgd,gjd->bgd', halves[:-1], weights[:, :STRIDE], precision=lax.Precision.HIGHEST)
    pooled = pooled + jnp.einsum('bjgd,gjd->bgd', halves[1:], weights[:, STRIDE:], precision=lax.Precision.HIGHEST)
    pooled = lax.optimization_barrier(pooled.astype(jnp.bfloat16)).astype(jnp.float32)
    summary = jnp.einsum('bgd,gde->bge', pooled, projection.astype(jnp.float32), precision=lax.Precision.HIGHEST)
    return summary.astype(jnp.bfloat16)

def soft_mix(scores, visible, value_rows):
    masked = jnp.where(visible, scores, -1e+30)
    highest = lax.optimization_barrier(jnp.max(masked, axis=-1, keepdims=True))
    weights = jnp.where(visible, jnp.exp(scores - highest), 0.0)
    weight_total = lax.optimization_barrier(jnp.sum(weights, axis=-1))
    rounded = lax.optimization_barrier(weights.astype(jnp.bfloat16)).astype(jnp.float32)
    numerator = jnp.einsum('tghs,sgd->tghd', rounded, value_rows, precision=lax.Precision.HIGHEST)
    safe_total = jnp.where(weight_total > 0.0, weight_total, 1.0)
    return numerator / safe_total[..., None]

def reference(queries, key_rows, values, gate_logits, key_mix, key_proj, value_mix, value_proj):
    per_group = QHEADS // GROUPS
    score_scale = 1.0 / math.sqrt(KDIM)
    keys_all = key_rows.reshape(TOKENS, GROUPS, KDIM)
    values_all = values.reshape(TOKENS, GROUPS, VDIM)
    summary_keys = compress_rows(keys_all, key_mix, key_proj).astype(jnp.float32)
    summary_values = compress_rows(values_all, value_mix, value_proj).astype(jnp.float32)
    padded_keys = jnp.concatenate([jnp.zeros((WINDOW, GROUPS, KDIM), keys_all.dtype), keys_all], 0)
    padded_values = jnp.concatenate([jnp.zeros((WINDOW, GROUPS, VDIM), values_all.dtype), values_all], 0)
    query_block = math.gcd(512, TOKENS)
    block_ends = jnp.arange(NBLOCKS, dtype=jnp.int32) * STRIDE + BLOCK - 1

    def one_block(block_index):
        first = (block_index * query_block).astype(jnp.int32)
        query_part = lax.dynamic_slice_in_dim(queries, first, query_block, 0)
        query_part = query_part.reshape(query_block, GROUPS, per_group, KDIM).astype(jnp.float32)
        gate_part = lax.dynamic_slice_in_dim(gate_logits, first, query_block, 0)
        gate_values = jax.nn.sigmoid(gate_part.reshape(query_block, GROUPS, per_group, 2).astype(jnp.float32))
        positions = first + jnp.arange(query_block, dtype=jnp.int32)
        scores = jnp.einsum('tghd,bgd->tghb', query_part, summary_keys, precision=lax.Precision.HIGHEST) * score_scale
        visible = (block_ends[None, :] <= positions[:, None])[:, None, None, :]
        compressed_out = soft_mix(scores, visible, summary_values)
        near_keys = lax.dynamic_slice_in_dim(padded_keys, first, query_block + WINDOW, 0).astype(jnp.float32)
        near_values = lax.dynamic_slice_in_dim(padded_values, first, query_block + WINDOW, 0).astype(jnp.float32)
        key_places = first - WINDOW + jnp.arange(query_block + WINDOW, dtype=jnp.int32)
        near_visible = (key_places[None, :] <= positions[:, None]) & (key_places[None, :] > positions[:, None] - WINDOW) & (key_places[None, :] >= 0)
        scores = jnp.einsum('tghd,sgd->tghs', query_part, near_keys, precision=lax.Precision.HIGHEST) * score_scale
        window_out = soft_mix(scores, near_visible[:, None, None, :], near_values)
        mixture = gate_values[..., 0:1] * compressed_out + gate_values[..., 1:2] * window_out
        return mixture.astype(jnp.bfloat16).reshape(query_block, QHEADS * VDIM)
    blocks = lax.map(one_block, jnp.arange(TOKENS // query_block, dtype=jnp.int32))
    return blocks.reshape(TOKENS, QHEADS * VDIM)
```

```python
import functools
import math

import jax
import jax.numpy as jnp
from jax import lax
from jax.experimental import pallas as pl
from jax.experimental.pallas import tpu as pltpu
from jax.sharding import PartitionSpec as P

BF = jnp.bfloat16
F32 = jnp.float32
MESH = pl.DeviceIdType.MESH
UNITS = 512
SCALE = 1.0 / math.sqrt(192.0)
NEG = -1e30


def where_am_i():
    ctx = lax.axis_index("ctx")
    x = lax.axis_index("head")
    z = ctx // 8
    y = (ctx // 2) % 4
    c = ctx % 2
    return ctx, x, z, y, c


def comm_kernel(
    kr, vr, kmix, kproj, vmix, vproj,
    win, comp,
    own, prev, mix, quad, col, zero,
    prev_s, prev_r, win_s, win_r, own_sem, quad_s, quad_r, z_s, z_r,
    a_s, a_r, b_s, b_r, d_s, d_r, loc_sem, zero_sem,
):
    ctx, x, z, y, c = where_am_i()
    unit = ctx * 4 + x
    par = x % 2
    half = x // 2
    group = 2 * c + par
    plane_base = z * 8

    def dev(v):
        return (v // 4, v % 4)

    ahead = jnp.minimum(8, UNITS - 1 - unit)
    behind = jnp.minimum(8, unit)

    barrier = pltpu.get_barrier_semaphore()

    def greet(device):
        pl.semaphore_signal(barrier, inc=1, device_id=device, device_id_type=MESH)

    lax.fori_loop(1, behind + 1, lambda d, k: (greet(dev(unit - d)), k)[1], 0)
    for m in range(1, 4):
        greet((ctx - c + (c + m // 2) % 2, x - par + (par + m % 2) % 2))
        greet((ctx, (x + m) % 4))
        greet((plane_base + ((y + m) % 4) * 2 + c, x))
    lax.fori_loop(0, z, lambda zz, k: (greet((ctx - 8 * (z - zz), x)), k)[1], 0)

    for g in range(4):
        own[g, :, 0:192] = kr[:, 192 * g:192 * g + 192]
        own[g, :, 192:256] = jnp.ones((64, 64), BF)
        own[g, :, 256:384] = vr[:, 128 * g:128 * g + 128]
        mix[g, :, 0:192] = kmix[g].astype(F32)
        mix[g, :, 192:256] = jnp.zeros((32, 64), F32)
        mix[g, :, 256:384] = vmix[g].astype(F32)

    def clear(zz, k):
        col[zz] = jnp.zeros((16, 384), BF)
        return k

    lax.fori_loop(z + 1, 16, clear, 0)
    zero[...] = jnp.zeros_like(zero)

    pl.semaphore_wait(barrier, ahead + 9 + 15 - z)

    def prev_copy(device):
        return pltpu.make_async_remote_copy(
            src_ref=own.at[:, 48:64, :], dst_ref=prev, send_sem=prev_s, recv_sem=prev_r,
            device_id=device, device_id_type=MESH)

    @pl.when(ahead > 0)
    def _():
        prev_copy(dev(unit + 1)).start()

    def win_copy(d, device):
        return pltpu.make_async_remote_copy(
            src_ref=own, dst_ref=win.at[:, 8 - d], send_sem=win_s.at[d - 1], recv_sem=win_r.at[d - 1],
            device_id=device, device_id_type=MESH)

    lax.fori_loop(1, ahead + 1, lambda d, k: (win_copy(d, dev(unit + d)).start(), k)[1], 0)
    own_copy = pltpu.make_async_copy(own, win.at[:, 8], own_sem)
    own_copy.start()

    def zero_copy(d):
        return pltpu.make_async_copy(zero, win.at[:, 8 - d], zero_sem.at[d - 1])

    lax.fori_loop(behind + 1, 9, lambda d, k: (zero_copy(d).start(), k)[1], 0)

    @pl.when(unit > 0)
    def _():
        prev_copy(dev(unit)).wait_recv()

    @pl.when(unit == 0)
    def _():
        prev[...] = jnp.zeros_like(prev)

    member = 2 * c + par
    row = lax.broadcasted_iota(jnp.int32, (16, 1), 0)
    mine = row // 4 == member
    lane = lax.broadcasted_iota(jnp.int32, (16, 384), 1)
    first = jnp.logical_and(unit == 0, row == 0)
    for g in range(4):
        rows = jnp.concatenate([prev[g].astype(F32), own[g].astype(F32)], 0).reshape(5, 16, 384)
        pooled = jnp.sum(rows[0:4] * mix[g, 0:16][None], axis=1)
        pooled = pooled + jnp.sum(rows[1:5] * mix[g, 16:32][None], axis=1)
        pooled = jnp.concatenate([pooled] * 4, 0)
        pooled = jnp.where(mine, pooled, 0.0).astype(BF)
        keys = jnp.dot(pooled[:, 0:192], kproj[g], preferred_element_type=F32)
        vals = jnp.dot(pooled[:, 256:384], vproj[g], preferred_element_type=F32)
        ones = jnp.where(jnp.logical_and(mine, jnp.logical_not(first)), 1.0, 0.0)
        keys = jnp.where(first, keys[1:2], keys)
        vals = jnp.where(first, 0.0, vals)
        tile = jnp.concatenate([keys, jnp.broadcast_to(ones, (16, 64)), vals], 1)
        quad[0, g] = tile.astype(BF)

    def quad_copy(g_to, m_from, device):
        return pltpu.make_async_remote_copy(
            src_ref=quad.at[0, g_to], dst_ref=quad.at[1, m_from], send_sem=quad_s.at[g_to],
            recv_sem=quad_r.at[m_from], device_id=device, device_id_type=MESH)

    for m in range(4):
        @pl.when(m != member)
        def _():
            quad_copy(m, member, (ctx - c + m // 2, x - par + m % 2)).start()
    for m in range(4):
        @pl.when(m != member)
        def _():
            quad_copy(m, m, (ctx, x)).wait_recv()
    total = quad[0, member].astype(F32)
    for m in range(4):
        total = total + jnp.where(m == member, 0.0, quad[1, m].astype(F32))
    col[z] = total.astype(BF)

    def z_copy(z_from, z_to):
        return pltpu.make_async_remote_copy(
            src_ref=col.at[z_from], dst_ref=col.at[z_from], send_sem=z_s.at[z_to],
            recv_sem=z_r.at[z_from], device_id=(z_to * 8 + y * 2 + c, x), device_id_type=MESH)

    lax.fori_loop(z + 1, 16, lambda zz, k: (z_copy(z, zz).start(), k)[1], 0)

    def z_wait(i, k):
        z_copy(z - 1 - i, z).wait_recv()
        return k

    lax.fori_loop(0, z, z_wait, 0)

    def peer_x(d):
        return (ctx, (x + d) % 4)

    def peer_y(d):
        return (plane_base + ((y + d) % 4) * 2 + c, x)

    def place(ci, g, yy, hh):
        return comp.at[g, pl.ds(4 * ci, 4), yy, hh]

    def a_copy(ci, d, yy, hh, gg):
        return pltpu.make_async_remote_copy(
            src_ref=col.at[pl.ds(4 * ci, 4)], dst_ref=place(ci, gg, yy, hh),
            send_sem=a_s.at[ci, d - 1], recv_sem=a_r.at[ci, d - 1],
            device_id=peer_x(d) if ci % 2 == 0 else peer_y(d), device_id_type=MESH)

    def from_a(ci, d):
        xx = (x + 4 - d) % 4 if ci % 2 == 0 else x
        yy = y if ci % 2 == 0 else (y + 4 - d) % 4
        return yy, xx // 2, 2 * c + xx % 2

    def b_ref(ci, xx, yy):
        if ci % 2 == 0:
            return comp.at[pl.ds(2 * c, 2), pl.ds(4 * ci, 4), yy]
        return comp.at[2 * c + xx % 2, pl.ds(4 * ci, 4), :, xx // 2]

    def b_copy(ci, d, xx, yy):
        ref = b_ref(ci, xx, yy)
        return pltpu.make_async_remote_copy(
            src_ref=ref, dst_ref=ref, send_sem=b_s.at[ci, d - 1], recv_sem=b_r.at[ci, d - 1],
            device_id=peer_y(d) if ci % 2 == 0 else peer_x(d), device_id_type=MESH)

    def d_copy(ci, cc):
        ref = comp.at[pl.ds(2 * cc, 2), pl.ds(4 * ci, 4)]
        return pltpu.make_async_remote_copy(
            src_ref=ref, dst_ref=ref, send_sem=d_s.at[ci], recv_sem=d_r.at[ci],
            device_id=(ctx - c + (1 - c), x), device_id_type=MESH)

    def own_place(ci):
        return pltpu.make_async_copy(col.at[pl.ds(4 * ci, 4)], place(ci, group, y, half), loc_sem.at[ci])

    for ci in (3, 2, 1, 0):
        @pl.when(4 * ci <= z)
        def _():
            own_place(ci).start()
            for d in (1, 3, 2):
                a_copy(ci, d, y, half, group).start()
    for ci in (3, 2, 1, 0):
        @pl.when(4 * ci <= z)
        def _():
            own_place(ci).wait()
            for d in (1, 3, 2):
                yy, hh, gg = from_a(ci, d)
                a_copy(ci, d, yy, hh, gg).wait_recv()
            for d in (1, 3, 2):
                b_copy(ci, d, x, y).start()
    for ci in (3, 2, 1, 0):
        @pl.when(4 * ci <= z)
        def _():
            for d in (1, 3, 2):
                if ci % 2 == 0:
                    b_copy(ci, d, x, (y + 4 - d) % 4).wait_recv()
                else:
                    b_copy(ci, d, (x + 4 - d) % 4, y).wait_recv()
            d_copy(ci, c).start()
    for ci in (3, 2, 1, 0):
        @pl.when(4 * ci <= z)
        def _():
            d_copy(ci, 1 - c).wait_recv()
            d_copy(ci, c).wait_send()
            for d in (1, 2, 3):
                a_copy(ci, d, y, half, group).wait_send()
                b_copy(ci, d, x, y).wait_send()

    lax.fori_loop(z + 1, 16, lambda zz, k: (z_copy(z, zz).wait_send(), k)[1], 0)
    for m in range(4):
        @pl.when(m != member)
        def _():
            quad_copy(m, member, (ctx, x)).wait_send()

    @pl.when(ahead > 0)
    def _():
        prev_copy(dev(unit)).wait_send()

    own_copy.wait()
    lax.fori_loop(behind + 1, 9, lambda d, k: (zero_copy(d).wait(), k)[1], 0)
    lax.fori_loop(1, ahead + 1, lambda d, k: (win_copy(d, dev(unit)).wait_send(), k)[1], 0)
    lax.fori_loop(1, behind + 1, lambda d, k: (win_copy(d, dev(unit)).wait_recv(), k)[1], 0)


def communicate(key_rows, values, key_mix, key_proj, value_mix, value_proj):
    dma = pltpu.SemaphoreType.DMA
    vmem = pl.BlockSpec(memory_space=pltpu.VMEM)
    return pl.pallas_call(
        comm_kernel,
        out_shape=(
            jax.ShapeDtypeStruct((4, 9, 64, 384), BF),
            jax.ShapeDtypeStruct((4, 16, 4, 2, 16, 384), BF),
        ),
        in_specs=[vmem] * 6,
        out_specs=(pl.BlockSpec(memory_space=pl.ANY), pl.BlockSpec(memory_space=pl.ANY)),
        scratch_shapes=[
            pltpu.VMEM((4, 64, 384), BF),
            pltpu.VMEM((4, 16, 384), BF),
            pltpu.VMEM((4, 32, 384), F32),
            pltpu.VMEM((2, 4, 16, 384), BF),
            pltpu.VMEM((16, 16, 384), BF),
            pltpu.VMEM((4, 64, 384), BF),
            dma, dma, dma((8,)), dma((8,)), dma, dma((4,)), dma((4,)), dma((16,)), dma((16,)),
            dma((4, 3)), dma((4, 3)), dma((4, 3)), dma((4, 3)), dma((4,)), dma((4,)), dma((4,)), dma((8,)),
        ],
        compiler_params=pltpu.CompilerParams(collective_id=0, has_side_effects=True, vmem_limit_bytes=32 * 2**20),
        cost_estimate=pl.CostEstimate(flops=10**8, bytes_accessed=10**7, transcendentals=0),
    )(key_rows, values, key_mix, key_proj, value_mix, value_proj)


RT = 512
KC = 1024


def attend_kernel(q_ref, g_ref, w_ref, c_ref, o_ref, qs, acc, mx, bw, bc, vlast):
    g = pl.program_id(0)
    ctx, x, z, y, c = where_am_i()
    unit = ctx * 4 + x
    nfull = z // 8
    lane = lax.broadcasted_iota(jnp.int32, (64, 256), 1)
    for h in range(16):
        j = h // 2
        if h % 2 == 0:
            t = q_ref[:, 384 * j:384 * j + 256]
            t = jnp.where(lane < 192, t, jnp.zeros_like(t))
        else:
            t = q_ref[:, 384 * j + 128:384 * j + 384].astype(F32)
            t = pltpu.roll(t, 192, 1)
            t = jnp.where(lane < 192, t, 0.0).astype(BF)
        qs[64 * h:64 * h + 64, :] = t

    @pl.when(g == 0)
    def _():
        i = lax.broadcasted_iota(jnp.int32, (64, 576), 0)
        k = lax.broadcasted_iota(jnp.int32, (64, 576), 1)
        seen = (k > i) & (k <= i + 512) & (k + 64 * (unit - 8) >= 0)
        bw[...] = jnp.where(seen, 0.0, NEG)
        i = lax.broadcasted_iota(jnp.int32, (64, KC), 0)
        k = lax.broadcasted_iota(jnp.int32, (64, KC), 1)
        zz = 8 * nfull + k // 128
        row = k % 128
        yy = row // 32
        hh = (row % 32) // 16
        m = (row % 16) // 4
        uu = 8 * (4 * zz + yy) + 4 * (m // 2) + 2 * hh + m % 2
        b = 4 * uu - 1 + row % 4
        seen = (16 * b + 31 <= 64 * unit + i) & (b >= 0)
        bc[...] = jnp.where(seen, 0.0, NEG)

    krow = lax.broadcasted_iota(jnp.int32, (KC, 384), 0)
    last = c_ref[0, pl.ds(pl.multiple_of(nfull * KC, KC), KC), :]
    vlast[...] = jnp.where(krow < 128 * (z % 8 + 1), last, jnp.zeros_like(last))
    sig = jax.nn.sigmoid(g_ref[...].astype(F32))
    sig = pltpu.roll(sig, lax.rem(128 - 32 * g, 128), 1)
    nh = RT // 64

    def scores(q, k):
        return lax.dot_general(q, k, (((1,), (1,)), ((), ())), preferred_element_type=F32)

    def tile(rt, carry):
        q = qs[pl.ds(pl.multiple_of(rt * RT, RT), RT), :]
        s = scores(q, w_ref[0, :, 0:256])
        s = (s.reshape(nh, 64, 576) + bw[...][None]).reshape(RT, 576)
        m = jnp.max(s, axis=1, keepdims=True)
        p = jnp.exp((s - m) * SCALE).astype(BF)
        aw = jnp.dot(p, w_ref[0, :, 128:384], preferred_element_type=F32)

        s = scores(q, vlast[:, 0:256])
        s = (s.reshape(nh, 64, KC) + bc[...][None]).reshape(RT, KC)
        m = jnp.maximum(jnp.max(s, axis=1, keepdims=True), -1e29)
        p = jnp.exp((s - m) * SCALE).astype(BF)
        acc[...] = jnp.dot(p, vlast[:, 128:384], preferred_element_type=F32)
        mx[...] = jnp.broadcast_to(m, (RT, 128))

        def step(i, k):
            rows = pl.ds(pl.multiple_of(i * KC, KC), KC)
            s = scores(q, c_ref[0, rows, 0:256])
            before = mx[:, 0:1]
            m = jnp.maximum(jnp.max(s, axis=1, keepdims=True), before)
            p = jnp.exp((s - m) * SCALE).astype(BF)
            factor = jnp.exp((before - m) * SCALE)
            acc[...] = acc[...] * factor + jnp.dot(p, c_ref[0, rows, 128:384], preferred_element_type=F32)
            mx[...] = jnp.broadcast_to(m, (RT, 128))
            return k

        lax.fori_loop(0, nfull, step, 0)
        ac = acc[...]
        lc = ac[:, 64:65]
        oc = ac[:, 128:256] / jnp.where(lc > 0.0, lc, 1.0)
        ow = aw[:, 128:256] / aw[:, 64:65]
        sg = pltpu.roll(sig, lax.rem(128 - 2 * nh * rt, 128), 1)
        for h in range(nh):
            r = slice(64 * h, 64 * h + 64)
            o = sg[:, 2 * h:2 * h + 1] * oc[r] + sg[:, 2 * h + 1:2 * h + 2] * ow[r]
            o_ref[:, pl.ds(pl.multiple_of((rt * nh + h) * 128, 128), 128)] = o.astype(BF)
        return carry

    lax.fori_loop(0, 1024 // RT, tile, 0)


def attend(queries, gates, win, comp):
    return pl.pallas_call(
        attend_kernel,
        grid=(4,),
        in_specs=[
            pl.BlockSpec((64, 3072), lambda g: (0, g)),
            pl.BlockSpec((64, 128), lambda g: (0, 0)),
            pl.BlockSpec((1, 576, 384), lambda g: (g, 0, 0)),
            pl.BlockSpec((1, 2048, 384), lambda g: (g, 0, 0)),
        ],
        out_specs=pl.BlockSpec((64, 2048), lambda g: (0, g)),
        out_shape=jax.ShapeDtypeStruct((64, 8192), BF),
        scratch_shapes=[
            pltpu.VMEM((1024, 256), BF), pltpu.VMEM((RT, 256), F32), pltpu.VMEM((RT, 128), F32),
            pltpu.VMEM((64, 576), F32), pltpu.VMEM((64, KC), F32), pltpu.VMEM((KC, 384), BF),
        ],
        compiler_params=pltpu.CompilerParams(vmem_limit_bytes=48 * 2**20),
    )(queries, gates, win, comp)


def local(queries, key_rows, values, gate_logits, key_mix, key_proj, value_mix, value_proj):
    win, comp = communicate(key_rows, values, key_mix, key_proj, value_mix, value_proj)
    return attend(queries, gate_logits, win.reshape(4, 576, 384), comp.reshape(4, 2048, 384))


def solution(mesh):
    rows = P(("ctx", "head"), None)
    return jax.shard_map(
        local, mesh=mesh, in_specs=(rows,) * 4 + (P(),) * 4, out_specs=rows, check_vma=False)
```

```python
import math

import jax
import jax.numpy as jnp
from jax import lax
from jax.experimental import pallas as pl
from jax.experimental.pallas import tpu as pltpu
from jax.sharding import PartitionSpec as P

BF = jnp.bfloat16
F32 = jnp.float32
MESH = pl.DeviceIdType.MESH
UNITS = 512
SCALE = 1.0 / math.sqrt(192.0)
NEG = -1e30
FLOOR = -1e29
RT = 512
KC = 1024
WK = 576


def loop(lower, upper, act):
    def body(i, carry):
        act(i)
        return carry

    lax.fori_loop(lower, upper, body, 0)


def fused_kernel(
    q_ref, kr, vr, gates, kmix, kproj, vmix, vproj,
    out,
    own, prev, mix, kp, quad, piece, win, comp, qs, gw, gc, vx, acc, mx, owin, s0, s1, bw, bc,
    prev_s, prev_r, win_s, win_r, own_sem, rel_s, rel_r, quad_s, quad_r, z_s, z_r,
    a_s, a_r, b_s, b_r, d_s, d_r,
):
    ctx = lax.axis_index("ctx")
    x = lax.axis_index("head")
    z = ctx // 8
    y = (ctx // 2) % 4
    c = ctx % 2
    row = ctx // 2
    unit = ctx * 4 + x
    par = x % 2
    half = x // 2
    member = 2 * c + par
    zp = (z + par + 1) % 2
    base = 8 * row + x - 8
    sibling = (ctx - c + (1 - c), x)

    def dev(v):
        return (v // 4, v % 4)

    def remote(src, dst, send, recv, device):
        return pltpu.make_async_remote_copy(
            src_ref=src, dst_ref=dst, send_sem=send, recv_sem=recv, device_id=device, device_id_type=MESH)

    barrier = pltpu.get_barrier_semaphore()

    def greet(device):
        pl.semaphore_signal(barrier, inc=1, device_id=device, device_id_type=MESH)

    def later(act):
        loop(0, (16 - z - par) // 2, lambda i: act(z + 2 * i + 2 - (1 - par)))

    def earlier(act):
        loop(0, (z + 1 - par) // 2, lambda i: act(z - 2 * i - 2 + (1 - par)))

    earlier(lambda zz: greet((zz * 8 + y * 2 + c, x)))

    @pl.when(unit > 0)
    def _():
        greet(dev(unit - 1))

    for m in range(1, 4):
        greet((ctx - c + (c + m // 2) % 2, x - par + (par + m % 2) % 2))
        greet((ctx, (x + m) % 4))
        greet((z * 8 + ((y + m) % 4) * 2 + c, x))
    greet(sibling)

    def source_slots(act):
        def one(s):
            @pl.when(jnp.logical_and(base + s >= 0, s != 8 + 4 * c))
            def _():
                act(s)

        loop(0, 13, one)

    source_slots(lambda s: greet(dev(base + s)))

    for h in range(2):
        own[h, :, 0:384] = kr[:, 384 * h:384 * h + 384]
        own[h, :, 384:640] = vr[:, 256 * h:256 * h + 256]
        mix[h, :, 0:192] = kmix[2 * h].astype(F32)
        mix[h, :, 192:384] = kmix[2 * h + 1].astype(F32)
        mix[h, :, 384:512] = vmix[2 * h].astype(F32)
        mix[h, :, 512:640] = vmix[2 * h + 1].astype(F32)
        kp[h] = jnp.zeros((384, 384), BF)
        kp[h, 0:192, 0:192] = kproj[2 * h]
        kp[h, 192:384, 192:384] = kproj[2 * h + 1]

    next_row = (row < 63).astype(jnp.int32)
    targets = jnp.where(c == 0, 7 + next_row * 2 * (x + 1), 2 * (3 - x) + 1 + next_row * 8)
    pl.semaphore_wait(
        barrier,
        targets + (unit < UNITS - 1).astype(jnp.int32) + 10 + (16 - z - par) // 2)

    def prev_copy(device):
        return remote(own.at[:, 48:64, :], prev, prev_s, prev_r, device)

    @pl.when(unit < UNITS - 1)
    def _():
        prev_copy(dev(unit + 1)).start()

    @pl.when(row == 0)
    def _():
        def clear(s):
            win[c, s] = jnp.zeros((64, 640), BF)

        loop(0, 8 - x, clear)

    def clear_plane(zz):
        @pl.when(zz % 2 == zp)
        def _():
            comp[c, zz // 2, zz % 2, y, half] = jnp.zeros((16, 640), BF)

    loop(z + 1, 4 * (z // 4) + 4, clear_plane)

    @pl.when((z // 4) % 2 == 0)
    def _():
        def clear(i):
            comp[:, 2 * (z // 4) + 2 + i] = jnp.zeros((2, 2, 4, 2, 16, 640), BF)

        loop(0, 2, clear)

    @pl.when(unit > 0)
    def _():
        prev_copy(dev(unit)).wait_recv()

    @pl.when(unit == 0)
    def _():
        prev[...] = jnp.zeros_like(prev)

    rows16 = lax.broadcasted_iota(jnp.int32, (16, 1), 0)
    mine = rows16 // 4 == member
    no_block = jnp.logical_and(unit == 0, rows16 == 0)
    for h in range(2):
        rows = jnp.concatenate([prev[h].astype(F32), own[h].astype(F32)], 0).reshape(5, 16, 640)
        pooled = jnp.sum(rows[0:4] * mix[h, 0:16][None], axis=1)
        pooled = pooled + jnp.sum(rows[1:5] * mix[h, 16:32][None], axis=1)
        pooled = jnp.concatenate([pooled] * 4, 0)
        pooled = jnp.where(mine, pooled, 0.0).astype(BF)
        keys = jnp.dot(pooled[:, 0:384], kp[h], preferred_element_type=F32)
        v0 = jnp.dot(pooled[:, 384:512], vproj[2 * h], preferred_element_type=F32)
        v1 = jnp.dot(pooled[:, 512:640], vproj[2 * h + 1], preferred_element_type=F32)
        keys = jnp.where(no_block, keys[1:2], keys)
        quad[0, h, :, 0:384] = keys.astype(BF)
        quad[0, h, :, 384:512] = jnp.where(no_block, 0.0, v0).astype(BF)
        quad[0, h, :, 512:640] = jnp.where(no_block, 0.0, v1).astype(BF)

    def quad_copy(m_to, m_from, device):
        return remote(
            quad.at[0, m_to // 2], quad.at[1 + m_from // 2, m_from % 2], quad_s.at[m_to], quad_r.at[m_from], device)

    for m in range(4):
        @pl.when(m != member)
        def _():
            quad_copy(m, member, (ctx - c + m // 2, x - par + m % 2)).start()
    for m in range(4):
        @pl.when(m != member)
        def _():
            quad_copy(m, m, (ctx, x)).wait_recv()
    total = quad[0, c].astype(F32)
    for m in range(4):
        total = total + jnp.where(m == member, 0.0, quad[1 + m // 2, m % 2].astype(F32))
    piece[...] = total.astype(BF)

    @pl.when(par == 1)
    def _():
        comp[c, z // 2, z % 2, y, half] = piece[...]

    def z_copy(z_from, z_to):
        ref = comp.at[c, z_from // 2, z_from % 2, y, half]
        return remote(piece, ref, z_s.at[z_to], z_r.at[z_from], (z_to * 8 + y * 2 + c, x))

    later(lambda zz: z_copy(z, zz).start())

    def win_copy(h, nxt, x_to, slot, device):
        return remote(own.at[h], win.at[h, slot], win_s.at[h, nxt, x_to], win_r.at[slot], device)

    def win_targets(act):
        for nxt in range(2):
            for m in range(4):
                x_to = (x + m) % 4
                slot = unit - (8 * (row + nxt) + x_to - 8)
                needed = jnp.logical_and(slot >= 0, slot <= 12)
                needed = jnp.logical_and(needed, row + nxt < 64)
                for h in range(2):
                    ctx_to = 2 * (row + nxt) + h
                    other = jnp.logical_or(ctx_to != ctx, x_to != x)

                    @pl.when(jnp.logical_and(needed, other))
                    def _():
                        act(win_copy(h, nxt, x_to, slot, (ctx_to, x_to)))

    win_targets(lambda copy: copy.start())
    own_copy = pltpu.make_async_copy(own.at[c], win.at[c, 8 + 4 * c], own_sem)
    own_copy.start()

    lane = lax.broadcasted_iota(jnp.int32, (64, 256), 1)
    zero = jnp.zeros((64, 256), F32)
    for head in range(64):
        g, hh = head // 16, head % 16
        at = 384 * (head // 2) + 128 * (head % 2)
        t = q_ref[:, at:at + 256].astype(F32)
        if head % 2 != g % 2:
            t = pltpu.roll(t, 192 if head % 2 else 64, 1)
        t = jnp.where(lane < 192 if g % 2 == 0 else lane >= 64, t, zero)
        qs[g, 64 * hh:64 * hh + 64, :] = t.astype(BF)
    sig = jax.nn.sigmoid(gates[...].astype(F32))
    for head in range(64):
        g, hh = head // 16, head % 16
        gc[g, 64 * hh:64 * hh + 64, :] = jnp.broadcast_to(sig[:, 2 * head:2 * head + 1], (64, 128))
        gw[g, 64 * hh:64 * hh + 64, :] = jnp.broadcast_to(sig[:, 2 * head + 1:2 * head + 2], (64, 128))
    vx[:, :, 128:256] = jnp.ones((4, KC, 128), BF)

    i = lax.broadcasted_iota(jnp.int32, (64, WK), 0)
    k = lax.broadcasted_iota(jnp.int32, (64, WK), 1)
    bw[...] = jnp.where((k > i) & (k <= i + 512) & (k + 64 * (unit - 8) >= 0), 0.0, NEG)
    last_chunk = z // 8
    i = lax.broadcasted_iota(jnp.int32, (64, KC), 0)
    k = lax.broadcasted_iota(jnp.int32, (64, KC), 1)
    r = k % 128
    m = (r % 16) // 4
    u = 8 * (4 * (8 * last_chunk + k // 128) + r // 32) + 4 * (m // 2) + 2 * ((r % 32) // 16) + m % 2
    b = 4 * u - 1 + r % 4
    bc[...] = jnp.where((16 * b + 31 <= 64 * unit + i) & (b >= 0), 0.0, NEG)

    earlier(lambda zz: z_copy(zz, z).wait_recv())

    def peer(along_x, d):
        if along_x:
            return (ctx, (x + d) % 4)
        return (z * 8 + ((y + d) % 4) * 2 + c, x)

    def a_copy(ci, d, xx, yy):
        pp = (z + xx % 2 + 1) % 2
        ref = comp.at[c, pl.ds(2 * ci, 2), pp, yy, xx // 2]
        return remote(ref, ref, a_s.at[ci, d - 1], a_r.at[ci, d - 1], peer(ci % 2 == 0, d))

    def b_copy(ci, d, xx, yy):
        if ci % 2 == 0:
            ref = comp.at[c, pl.ds(2 * ci, 2), :, yy]
        else:
            ref = comp.at[c, pl.ds(2 * ci, 2), (z + xx % 2 + 1) % 2, :, xx // 2]
        return remote(ref, ref, b_s.at[ci, d - 1], b_r.at[ci, d - 1], peer(ci % 2 == 1, d))

    def d_copy(ci, cc):
        ref = comp.at[cc, pl.ds(2 * ci, 2)]
        return remote(ref, ref, d_s.at[ci], d_r.at[ci], sibling)

    def back(along_x, d):
        return ((x + 4 - d) % 4, y) if along_x else (x, (y + 4 - d) % 4)

    def chunks(which, act):
        for ci in which:
            @pl.when(4 * ci <= z)
            def _():
                act(ci)

    def send_a(ci):
        for d in (1, 3, 2):
            a_copy(ci, d, x, y).start()

    def send_b(ci):
        for d in (1, 3, 2):
            a_copy(ci, d, *back(ci % 2 == 0, d)).wait_recv()
        for d in (1, 3, 2):
            b_copy(ci, d, x, y).start()

    def send_d(ci):
        for d in (1, 3, 2):
            b_copy(ci, d, *back(ci % 2 == 1, d)).wait_recv()
        d_copy(ci, c).start()

    chunks((3, 2, 1, 0), send_a)

    def win_wait(s):
        remote(own.at[0], win.at[c, s], win_s.at[0, 0, 0], win_r.at[s], sibling).wait_recv()

    source_slots(win_wait)
    own_copy.wait()

    def relay(cc, first):
        ref = win.at[cc, pl.ds(4 * first, 9)]
        return remote(ref, ref, rel_s, rel_r, sibling)

    relay(c, 1 - c).start()
    relay(1 - c, c).wait_recv()

    def scores(g, tile, keys):
        q = qs[g, pl.ds(pl.multiple_of(tile * RT, RT), RT), :]
        return lax.dot_general(q, keys, (((1,), (1,)), ((), ())), preferred_element_type=F32)

    def biased(s, bias):
        width = s.shape[1]
        return (s.reshape(RT // 64, 64, width) + bias[...][None]).reshape(RT, width)

    def win_keys(h, odd):
        return win[h, pl.ds(4 * c, 9), :, 128 * odd:128 * odd + 256].reshape(WK, 256)

    def win_done(s, g, tile):
        rows = pl.ds(pl.multiple_of(tile * RT, RT), RT)
        s = biased(s, bw)
        top = jnp.max(s, axis=1, keepdims=True)
        p = jnp.exp((s - top) * SCALE).astype(BF)
        a = jnp.dot(p, vx[g, 0:WK, :], preferred_element_type=F32)
        owin[g, rows, :] = gw[g, rows, :] * a[:, 0:128] / a[:, 128:256]

    def comp_keys(h, odd, chunk):
        return comp[h, pl.ds(4 * chunk, 4), :, :, :, :, 128 * odd:128 * odd + 256].reshape(KC, 256)

    def comp_done(s, g, tile, first):
        rows = pl.ds(pl.multiple_of(tile * RT, RT), RT)
        if first:
            s = biased(s, bc)
            top = jnp.maximum(jnp.max(s, axis=1, keepdims=True), FLOOR)
            p = jnp.exp((s - top) * SCALE).astype(BF)
            acc[g, rows, :] = jnp.dot(p, vx[g], preferred_element_type=F32)
        else:
            before = mx[g, rows, 0:1]
            top = jnp.maximum(jnp.max(s, axis=1, keepdims=True), before)
            p = jnp.exp((s - top) * SCALE).astype(BF)
            factor = jnp.exp((before - top) * SCALE)
            acc[g, rows, :] = acc[g, rows, :] * factor + jnp.dot(p, vx[g], preferred_element_type=F32)
        mx[g, rows, :] = jnp.broadcast_to(top, (RT, 128))

    tiles = 1024 // RT

    def run_half(h, width, keys, done):
        s0[:, 0:width] = scores(2 * h, 0, keys(h, 0))

        def body(t):
            s1[:, 0:width] = scores(2 * h + 1, t, keys(h, 1))
            done(s0[:, 0:width], 2 * h, t)
            s0[:, 0:width] = scores(2 * h, jnp.minimum(t + 1, tiles - 1), keys(h, 0))
            done(s1[:, 0:width], 2 * h + 1, t)

        loop(0, tiles, body)

    for g in range(4):
        vx[g, 0:WK, 0:128] = win[
            g // 2, pl.ds(4 * c, 9), :, 384 + 128 * (g % 2):512 + 128 * (g % 2)].reshape(WK, 128)
    run_half(0, WK, win_keys, win_done)
    chunks((3, 2, 1, 0), send_b)
    run_half(1, WK, win_keys, win_done)

    def load_values(chunk):
        for g in range(4):
            at = 384 + 128 * (g % 2)
            vx[g, :, 0:128] = comp[g // 2, pl.ds(4 * chunk, 4), :, :, :, :, at:at + 128].reshape(KC, 128)
        weight = jnp.where(jnp.logical_and(chunk == 0, rows16 == 0), 0.0, 1.0).astype(BF)
        for g in range(4):
            vx[g, 0:16, 128:256] = jnp.broadcast_to(weight, (16, 128))

    def ready(which):
        chunks(which, send_d)
        chunks(which, lambda ci: d_copy(ci, 1 - c).wait_recv())

    @pl.when(z >= 8)
    def _():
        ready((3, 2))

    @pl.when(z < 8)
    def _():
        ready((1, 0))

    load_values(last_chunk)

    def first_pass(h):
        run_half(h, KC, lambda hh, odd: comp_keys(hh, odd, last_chunk),
                 lambda s, g, t: comp_done(s, g, t, True))

    loop(0, 2, first_pass)

    @pl.when(z >= 8)
    def _():
        ready((1, 0))
        load_values(jnp.int32(0))
        loop(0, 2, lambda h: run_half(
            h, KC, lambda hh, odd: comp_keys(hh, odd, 0), lambda s, g, t: comp_done(s, g, t, False)))

    for g in range(4):
        for hh in range(16):
            rows = slice(64 * hh, 64 * hh + 64)
            weight = acc[g, rows, 128:256]
            o = gc[g, rows, :] * acc[g, rows, 0:128] / jnp.where(weight > 0.0, weight, 1.0) + owin[g, rows, :]
            at = 128 * (16 * g + hh)
            out[:, at:at + 128] = o.astype(BF)

    def sent(ci):
        d_copy(ci, c).wait_send()
        for d in (1, 2, 3):
            a_copy(ci, d, x, y).wait_send()
            b_copy(ci, d, x, y).wait_send()

    chunks((3, 2, 1, 0), sent)
    relay(c, 1 - c).wait_send()
    win_targets(lambda copy: copy.wait_send())
    later(lambda zz: z_copy(z, zz).wait_send())
    for m in range(4):
        @pl.when(m != member)
        def _():
            quad_copy(m, member, (ctx, x)).wait_send()

    @pl.when(unit < UNITS - 1)
    def _():
        prev_copy(dev(unit)).wait_send()


def local(queries, key_rows, values, gate_logits, key_mix, key_proj, value_mix, value_proj):
    dma = pltpu.SemaphoreType.DMA
    vmem = pl.BlockSpec(memory_space=pltpu.VMEM)
    return pl.pallas_call(
        fused_kernel,
        out_shape=jax.ShapeDtypeStruct((64, 8192), BF),
        in_specs=[vmem] * 8,
        out_specs=vmem,
        scratch_shapes=[
            pltpu.VMEM((2, 64, 640), BF),
            pltpu.VMEM((2, 16, 640), BF),
            pltpu.VMEM((2, 32, 640), F32),
            pltpu.VMEM((2, 384, 384), BF),
            pltpu.VMEM((3, 2, 16, 640), BF),
            pltpu.VMEM((16, 640), BF),
            pltpu.VMEM((2, 13, 64, 640), BF),
            pltpu.VMEM((2, 8, 2, 4, 2, 16, 640), BF),
            pltpu.VMEM((4, 1024, 256), BF),
            pltpu.VMEM((4, 1024, 128), F32),
            pltpu.VMEM((4, 1024, 128), F32),
            pltpu.VMEM((4, KC, 256), BF),
            pltpu.VMEM((4, 1024, 256), F32),
            pltpu.VMEM((4, 1024, 128), F32),
            pltpu.VMEM((4, 1024, 128), F32),
            pltpu.VMEM((RT, KC), F32),
            pltpu.VMEM((RT, KC), F32),
            pltpu.VMEM((64, WK), F32),
            pltpu.VMEM((64, KC), F32),
            dma, dma, dma((2, 2, 4)), dma((13,)), dma, dma, dma, dma((4,)), dma((4,)), dma((16,)), dma((16,)),
            dma((4, 3)), dma((4, 3)), dma((4, 3)), dma((4, 3)), dma((4,)), dma((4,)),
        ],
        compiler_params=pltpu.CompilerParams(
            collective_id=0, has_side_effects=True, vmem_limit_bytes=56 * 2**20),
        cost_estimate=pl.CostEstimate(flops=10**10, bytes_accessed=10**7, transcendentals=10**7),
    )(queries, key_rows, values, gate_logits, key_mix, key_proj, value_mix, value_proj)


def solution(mesh):
    rows = P(("ctx", "head"), None)
    return jax.shard_map(
        local, mesh=mesh, in_specs=(rows,) * 4 + (P(),) * 4, out_specs=rows, check_vma=False)
```

```python
import math

import jax
import jax.numpy as jnp
from jax import lax
from jax.experimental import pallas as pl
from jax.experimental.pallas import tpu as pltpu
from jax.sharding import PartitionSpec as P

BF = jnp.bfloat16
F32 = jnp.float32
MESH = pl.DeviceIdType.MESH
UNITS = 512
SCALE = 1.0 / math.sqrt(192.0)
NEG = -1e30
FLOOR = -1e29
RT = 512
KC = 1024
WK = 576


def loop(lower, upper, act):
    def body(i, carry):
        act(i)
        return carry

    lax.fori_loop(lower, upper, body, 0)


def fused_kernel(
    q_any, kr, vr, gates, kmix, kproj, vmix, vproj,
    out,
    q_ref, own, prev, mix, kp, quad, piece, win, comp, qs, gw, gc, vx, acc, mx, owin, s0, s1, bw, bc,
    q_sem, prev_s, prev_r, win_s, win_r, own_sem, rel_s, rel_r, quad_s, quad_r, z_s, z_r,
    a_s, a_r, b_s, b_r, d_s, d_r,
):
    q_copy = pltpu.make_async_copy(q_any, q_ref, q_sem)
    q_copy.start()
    ctx = lax.axis_index("ctx")
    x = lax.axis_index("head")
    z = ctx // 8
    y = (ctx // 2) % 4
    c = ctx % 2
    row = ctx // 2
    unit = ctx * 4 + x
    par = x % 2
    half = x // 2
    member = 2 * c + par
    zp = (z + par + 1) % 2
    base = 8 * row + x - 8
    sibling = (ctx - c + (1 - c), x)

    def dev(v):
        return (v // 4, v % 4)

    def remote(src, dst, send, recv, device):
        return pltpu.make_async_remote_copy(
            src_ref=src, dst_ref=dst, send_sem=send, recv_sem=recv, device_id=device, device_id_type=MESH)

    barrier = pltpu.get_barrier_semaphore()

    def greet(device):
        pl.semaphore_signal(barrier, inc=1, device_id=device, device_id_type=MESH)

    def later(act):
        loop(0, (16 - z - par) // 2, lambda i: act(z + 2 * i + 2 - (1 - par)))

    def earlier(act):
        loop(0, (z + 1 - par) // 2, lambda i: act(z - 2 * i - 2 + (1 - par)))

    earlier(lambda zz: greet((zz * 8 + y * 2 + c, x)))

    @pl.when(unit > 0)
    def _():
        greet(dev(unit - 1))

    for m in range(1, 4):
        greet((ctx - c + (c + m // 2) % 2, x - par + (par + m % 2) % 2))
        greet((ctx, (x + m) % 4))
        greet((z * 8 + ((y + m) % 4) * 2 + c, x))
    greet(sibling)

    def source_slots(act):
        def one(s):
            @pl.when(jnp.logical_and(base + s >= 0, s != 8 + 4 * c))
            def _():
                act(s)

        loop(0, 13, one)

    source_slots(lambda s: greet(dev(base + s)))

    for h in range(2):
        own[h, :, 0:384] = kr[:, 384 * h:384 * h + 384]
        own[h, :, 384:640] = vr[:, 256 * h:256 * h + 256]
        mix[h, :, 0:192] = kmix[2 * h].astype(F32)
        mix[h, :, 192:384] = kmix[2 * h + 1].astype(F32)
        mix[h, :, 384:512] = vmix[2 * h].astype(F32)
        mix[h, :, 512:640] = vmix[2 * h + 1].astype(F32)
        kp[h] = jnp.zeros((384, 384), BF)
        kp[h, 0:192, 0:192] = kproj[2 * h]
        kp[h, 192:384, 192:384] = kproj[2 * h + 1]

    next_row = (row < 63).astype(jnp.int32)
    targets = jnp.where(c == 0, 7 + next_row * 2 * (x + 1), 2 * (3 - x) + 1 + next_row * 8)
    pl.semaphore_wait(
        barrier,
        targets + (unit < UNITS - 1).astype(jnp.int32) + 10 + (16 - z - par) // 2)

    def prev_copy(device):
        return remote(own.at[:, 48:64, :], prev, prev_s, prev_r, device)

    @pl.when(unit < UNITS - 1)
    def _():
        prev_copy(dev(unit + 1)).start()

    def win_copy(h, nxt, x_to, slot, device):
        return remote(own.at[h], win.at[h, slot], win_s.at[h, nxt, x_to], win_r.at[slot], device)

    def win_targets(act):
        for nxt in range(2):
            for m in range(4):
                x_to = (x + m) % 4
                slot = unit - (8 * (row + nxt) + x_to - 8)
                needed = jnp.logical_and(slot >= 0, slot <= 12)
                needed = jnp.logical_and(needed, row + nxt < 64)
                for h in range(2):
                    ctx_to = 2 * (row + nxt) + h
                    other = jnp.logical_or(ctx_to != ctx, x_to != x)

                    @pl.when(jnp.logical_and(needed, other))
                    def _():
                        act(win_copy(h, nxt, x_to, slot, (ctx_to, x_to)))

    win_targets(lambda copy: copy.start())
    own_copy = pltpu.make_async_copy(own.at[c], win.at[c, 8 + 4 * c], own_sem)
    own_copy.start()

    @pl.when(row == 0)
    def _():
        def clear(s):
            win[c, s] = jnp.zeros((64, 640), BF)

        loop(0, 8 - x, clear)

    def clear_plane(zz):
        @pl.when(zz % 2 == zp)
        def _():
            comp[c, zz // 2, zz % 2, y, half] = jnp.zeros((16, 640), BF)

    loop(z + 1, 4 * (z // 4) + 4, clear_plane)

    @pl.when((z // 4) % 2 == 0)
    def _():
        def clear(i):
            comp[:, 2 * (z // 4) + 2 + i] = jnp.zeros((2, 2, 4, 2, 16, 640), BF)

        loop(0, 2, clear)

    @pl.when(unit > 0)
    def _():
        prev_copy(dev(unit)).wait_recv()

    @pl.when(unit == 0)
    def _():
        prev[...] = jnp.zeros_like(prev)

    rows16 = lax.broadcasted_iota(jnp.int32, (16, 1), 0)
    mine = rows16 // 4 == member
    no_block = jnp.logical_and(unit == 0, rows16 == 0)
    for h in range(2):
        rows = jnp.concatenate([prev[h].astype(F32), own[h].astype(F32)], 0).reshape(5, 16, 640)
        pooled = jnp.sum(rows[0:4] * mix[h, 0:16][None], axis=1)
        pooled = pooled + jnp.sum(rows[1:5] * mix[h, 16:32][None], axis=1)
        pooled = jnp.concatenate([pooled] * 4, 0)
        pooled = jnp.where(mine, pooled, 0.0).astype(BF)
        keys = jnp.dot(pooled[:, 0:384], kp[h], preferred_element_type=F32)
        v0 = jnp.dot(pooled[:, 384:512], vproj[2 * h], preferred_element_type=F32)
        v1 = jnp.dot(pooled[:, 512:640], vproj[2 * h + 1], preferred_element_type=F32)
        keys = jnp.where(no_block, keys[1:2], keys)
        quad[0, h, :, 0:384] = keys.astype(BF)
        quad[0, h, :, 384:512] = jnp.where(no_block, 0.0, v0).astype(BF)
        quad[0, h, :, 512:640] = jnp.where(no_block, 0.0, v1).astype(BF)

    def quad_copy(m_to, m_from, device):
        return remote(
            quad.at[0, m_to // 2], quad.at[1 + m_from // 2, m_from % 2], quad_s.at[m_to], quad_r.at[m_from], device)

    for m in range(4):
        @pl.when(m != member)
        def _():
            quad_copy(m, member, (ctx - c + m // 2, x - par + m % 2)).start()
    for m in range(4):
        @pl.when(m != member)
        def _():
            quad_copy(m, m, (ctx, x)).wait_recv()
    total = quad[0, c].astype(F32)
    for m in range(4):
        total = total + jnp.where(m == member, 0.0, quad[1 + m // 2, m % 2].astype(F32))
    piece[...] = total.astype(BF)

    @pl.when(par == 1)
    def _():
        comp[c, z // 2, z % 2, y, half] = piece[...]

    def z_copy(z_from, z_to):
        ref = comp.at[c, z_from // 2, z_from % 2, y, half]
        return remote(piece, ref, z_s.at[z_to], z_r.at[z_from], (z_to * 8 + y * 2 + c, x))

    later(lambda zz: z_copy(z, zz).start())

    lane = lax.broadcasted_iota(jnp.int32, (64, 256), 1)
    zero = jnp.zeros((64, 256), F32)
    q_copy.wait()
    for head in range(64):
        g, hh = head // 16, head % 16
        at = 384 * (head // 2) + 128 * (head % 2)
        t = q_ref[:, at:at + 256].astype(F32)
        if head % 2 != g % 2:
            t = pltpu.roll(t, 192 if head % 2 else 64, 1)
        t = jnp.where(lane < 192 if g % 2 == 0 else lane >= 64, t, zero)
        qs[g, 64 * hh:64 * hh + 64, :] = t.astype(BF)
    sig = jax.nn.sigmoid(gates[...].astype(F32))
    for head in range(64):
        g, hh = head // 16, head % 16
        gc[g, 64 * hh:64 * hh + 64, :] = jnp.broadcast_to(sig[:, 2 * head:2 * head + 1], (64, 128))
        gw[g, 64 * hh:64 * hh + 64, :] = jnp.broadcast_to(sig[:, 2 * head + 1:2 * head + 2], (64, 128))
    vx[:, :, 128:256] = jnp.ones((4, KC, 128), BF)

    i = lax.broadcasted_iota(jnp.int32, (64, WK), 0)
    k = lax.broadcasted_iota(jnp.int32, (64, WK), 1)
    bw[...] = jnp.where((k > i) & (k <= i + 512) & (k + 64 * (unit - 8) >= 0), 0.0, NEG)
    last_chunk = z // 8
    i = lax.broadcasted_iota(jnp.int32, (64, KC), 0)
    k = lax.broadcasted_iota(jnp.int32, (64, KC), 1)
    r = k % 128
    m = (r % 16) // 4
    u = 8 * (4 * (8 * last_chunk + k // 128) + r // 32) + 4 * (m // 2) + 2 * ((r % 32) // 16) + m % 2
    b = 4 * u - 1 + r % 4
    bc[...] = jnp.where((16 * b + 31 <= 64 * unit + i) & (b >= 0), 0.0, NEG)

    earlier(lambda zz: z_copy(zz, z).wait_recv())

    def peer(along_x, d):
        if along_x:
            return (ctx, (x + d) % 4)
        return (z * 8 + ((y + d) % 4) * 2 + c, x)

    def a_copy(ci, d, xx, yy):
        pp = (z + xx % 2 + 1) % 2
        ref = comp.at[c, pl.ds(2 * ci, 2), pp, yy, xx // 2]
        return remote(ref, ref, a_s.at[ci, d - 1], a_r.at[ci, d - 1], peer(ci % 2 == 0, d))

    def b_copy(ci, d, xx, yy):
        if ci % 2 == 0:
            ref = comp.at[c, pl.ds(2 * ci, 2), :, yy]
        else:
            ref = comp.at[c, pl.ds(2 * ci, 2), (z + xx % 2 + 1) % 2, :, xx // 2]
        return remote(ref, ref, b_s.at[ci, d - 1], b_r.at[ci, d - 1], peer(ci % 2 == 1, d))

    def d_copy(ci, cc):
        ref = comp.at[cc, pl.ds(2 * ci, 2)]
        return remote(ref, ref, d_s.at[ci], d_r.at[ci], sibling)

    def back(along_x, d):
        return ((x + 4 - d) % 4, y) if along_x else (x, (y + 4 - d) % 4)

    def chunks(which, act):
        for ci in which:
            @pl.when(4 * ci <= z)
            def _():
                act(ci)

    def send_a(ci):
        for d in (1, 3, 2):
            a_copy(ci, d, x, y).start()

    def send_b(ci):
        for d in (1, 3, 2):
            a_copy(ci, d, *back(ci % 2 == 0, d)).wait_recv()
        for d in (1, 3, 2):
            b_copy(ci, d, x, y).start()

    def send_d(ci):
        for d in (1, 3, 2):
            b_copy(ci, d, *back(ci % 2 == 1, d)).wait_recv()
        d_copy(ci, c).start()

    chunks((3, 2, 1, 0), send_a)

    def win_wait(s):
        remote(own.at[0], win.at[c, s], win_s.at[0, 0, 0], win_r.at[s], sibling).wait_recv()

    source_slots(win_wait)
    own_copy.wait()

    def relay(cc, first):
        ref = win.at[cc, pl.ds(4 * first, 9)]
        return remote(ref, ref, rel_s, rel_r, sibling)

    relay(c, 1 - c).start()

    def scores(g, tile, keys):
        q = qs[g, pl.ds(pl.multiple_of(tile * RT, RT), RT), :]
        return lax.dot_general(q, keys, (((1,), (1,)), ((), ())), preferred_element_type=F32)

    def biased(s, bias):
        width = s.shape[1]
        return (s.reshape(RT // 64, 64, width) + bias[...][None]).reshape(RT, width)

    def win_keys(h, odd):
        return win[h, pl.ds(4 * c, 9), :, 128 * odd:128 * odd + 256].reshape(WK, 256)

    def win_done(s, g, tile):
        rows = pl.ds(pl.multiple_of(tile * RT, RT), RT)
        s = biased(s, bw)
        top = jnp.max(s, axis=1, keepdims=True)
        p = jnp.exp((s - top) * SCALE).astype(BF)
        a = jnp.dot(p, vx[g, 0:WK, :], preferred_element_type=F32)
        owin[g, rows, :] = gw[g, rows, :] * a[:, 0:128] / a[:, 128:256]

    def comp_keys(h, odd, chunk):
        return comp[h, pl.ds(4 * chunk, 4), :, :, :, :, 128 * odd:128 * odd + 256].reshape(KC, 256)

    def comp_done(s, g, tile, first):
        rows = pl.ds(pl.multiple_of(tile * RT, RT), RT)
        if first:
            s = biased(s, bc)
            top = jnp.maximum(jnp.max(s, axis=1, keepdims=True), FLOOR)
            p = jnp.exp((s - top) * SCALE).astype(BF)
            acc[g, rows, :] = jnp.dot(p, vx[g], preferred_element_type=F32)
        else:
            before = mx[g, rows, 0:1]
            top = jnp.maximum(jnp.max(s, axis=1, keepdims=True), before)
            p = jnp.exp((s - top) * SCALE).astype(BF)
            factor = jnp.exp((before - top) * SCALE)
            acc[g, rows, :] = acc[g, rows, :] * factor + jnp.dot(p, vx[g], preferred_element_type=F32)
        mx[g, rows, :] = jnp.broadcast_to(top, (RT, 128))

    tiles = 1024 // RT

    def run_half(h, width, keys, done):
        s0[:, 0:width] = scores(2 * h, 0, keys(h, 0))

        def body(t):
            s1[:, 0:width] = scores(2 * h + 1, t, keys(h, 1))
            done(s0[:, 0:width], 2 * h, t)
            s0[:, 0:width] = scores(2 * h, jnp.minimum(t + 1, tiles - 1), keys(h, 0))
            done(s1[:, 0:width], 2 * h + 1, t)

        loop(0, tiles, body)

    def win_half(h):
        for odd in range(2):
            at = 384 + 128 * odd
            vx[2 * h + odd, 0:WK, 0:128] = win[h, pl.ds(4 * c, 9), :, at:at + 128].reshape(WK, 128)
        run_half(h, WK, win_keys, win_done)

    def comp_half(h, chunk, first):
        for odd in range(2):
            at = 384 + 128 * odd
            vx[2 * h + odd, :, 0:128] = comp[h, pl.ds(4 * chunk, 4), :, :, :, :, at:at + 128].reshape(KC, 128)
        weight = jnp.where(jnp.logical_and(chunk == 0, rows16 == 0), 0.0, 1.0).astype(BF)
        for odd in range(2):
            vx[2 * h + odd, 0:16, 128:256] = jnp.broadcast_to(weight, (16, 128))
        run_half(h, KC, lambda hh, odd: comp_keys(hh, odd, chunk),
                 lambda s, g, t: comp_done(s, g, t, first))

    def nearest(act):
        @pl.when(z >= 8)
        def _():
            chunks((3, 2), act)

        @pl.when(z < 8)
        def _():
            chunks((1, 0), act)

    def farther(act):
        @pl.when(z >= 8)
        def _():
            chunks((1, 0), act)

    def wait_d(ci):
        d_copy(ci, 1 - c).wait_recv()

    win_half(c)
    nearest(send_b)
    relay(1 - c, c).wait_recv()
    win_half(1 - c)
    nearest(send_d)
    farther(send_b)
    comp_half(c, last_chunk, True)
    nearest(wait_d)
    comp_half(1 - c, last_chunk, True)
    farther(send_d)

    @pl.when(z >= 8)
    def _():
        comp_half(c, jnp.int32(0), False)

    farther(wait_d)

    @pl.when(z >= 8)
    def _():
        comp_half(1 - c, jnp.int32(0), False)

    for g in range(4):
        for hh in range(16):
            rows = slice(64 * hh, 64 * hh + 64)
            weight = acc[g, rows, 128:256]
            o = gc[g, rows, :] * acc[g, rows, 0:128] / jnp.where(weight > 0.0, weight, 1.0) + owin[g, rows, :]
            at = 128 * (16 * g + hh)
            out[:, at:at + 128] = o.astype(BF)

    def sent(ci):
        d_copy(ci, c).wait_send()
        for d in (1, 2, 3):
            a_copy(ci, d, x, y).wait_send()
            b_copy(ci, d, x, y).wait_send()

    chunks((3, 2, 1, 0), sent)
    relay(c, 1 - c).wait_send()
    win_targets(lambda copy: copy.wait_send())
    later(lambda zz: z_copy(z, zz).wait_send())
    for m in range(4):
        @pl.when(m != member)
        def _():
            quad_copy(m, member, (ctx, x)).wait_send()

    @pl.when(unit < UNITS - 1)
    def _():
        prev_copy(dev(unit)).wait_send()


def local(queries, key_rows, values, gate_logits, key_mix, key_proj, value_mix, value_proj):
    dma = pltpu.SemaphoreType.DMA
    vmem = pl.BlockSpec(memory_space=pltpu.VMEM)
    return pl.pallas_call(
        fused_kernel,
        out_shape=jax.ShapeDtypeStruct((64, 8192), BF),
        in_specs=[pl.BlockSpec(memory_space=pl.ANY)] + [vmem] * 7,
        out_specs=vmem,
        scratch_shapes=[
            pltpu.VMEM((64, 12288), BF),
            pltpu.VMEM((2, 64, 640), BF),
            pltpu.VMEM((2, 16, 640), BF),
            pltpu.VMEM((2, 32, 640), F32),
            pltpu.VMEM((2, 384, 384), BF),
            pltpu.VMEM((3, 2, 16, 640), BF),
            pltpu.VMEM((16, 640), BF),
            pltpu.VMEM((2, 13, 64, 640), BF),
            pltpu.VMEM((2, 8, 2, 4, 2, 16, 640), BF),
            pltpu.VMEM((4, 1024, 256), BF),
            pltpu.VMEM((4, 1024, 128), F32),
            pltpu.VMEM((4, 1024, 128), F32),
            pltpu.VMEM((4, KC, 256), BF),
            pltpu.VMEM((4, 1024, 256), F32),
            pltpu.VMEM((4, 1024, 128), F32),
            pltpu.VMEM((4, 1024, 128), F32),
            pltpu.VMEM((RT, KC), F32),
            pltpu.VMEM((RT, KC), F32),
            pltpu.VMEM((64, WK), F32),
            pltpu.VMEM((64, KC), F32),
            dma, dma, dma, dma((2, 2, 4)), dma((13,)), dma, dma, dma, dma((4,)), dma((4,)), dma((16,)), dma((16,)),
            dma((4, 3)), dma((4, 3)), dma((4, 3)), dma((4, 3)), dma((4,)), dma((4,)),
        ],
        compiler_params=pltpu.CompilerParams(
            collective_id=0, has_side_effects=True, vmem_limit_bytes=56 * 2**20),
        cost_estimate=pl.CostEstimate(flops=10**10, bytes_accessed=10**7, transcendentals=10**7),
    )(queries, key_rows, values, gate_logits, key_mix, key_proj, value_mix, value_proj)


def solution(mesh):
    rows = P(("ctx", "head"), None)
    return jax.shard_map(
        local, mesh=mesh, in_specs=(rows,) * 4 + (P(),) * 4, out_specs=rows, check_vma=False)
```

```python
import math

import jax
import jax.numpy as jnp
from jax import lax
from jax.experimental import pallas as pl
from jax.experimental.pallas import tpu as pltpu
from jax.sharding import PartitionSpec as P

BF = jnp.bfloat16
F32 = jnp.float32
MESH = pl.DeviceIdType.MESH
UNITS = 512
SCALE = 1.0 / math.sqrt(192.0)
NEG = -1e30
FLOOR = -1e29
RT = 512
KC = 1024
WK = 576


def loop(lower, upper, act):
    def body(i, carry):
        act(i)
        return carry

    lax.fori_loop(lower, upper, body, 0)


def fused_kernel(
    q_any, kr, vr, gates, kmix, kproj, vmix, vproj,
    out,
    q_ref, own, mix, kp, tile, tail, quad, tail_in, piece, win, comp, qs, gw, gc, vx, acc, mx, owin, s0, s1, bw, bc,
    q_sem, tail_s, tail_r, win_s, win_r, own_sem, rel_s, rel_r, quad_s, quad_r, z_s, z_r,
    a_s, a_r, b_s, b_r, d_s, d_r, pass_s,
):
    q_copy = pltpu.make_async_copy(q_any, q_ref, q_sem)
    q_copy.start()
    ctx = lax.axis_index("ctx")
    x = lax.axis_index("head")
    z = ctx // 8
    y = (ctx // 2) % 4
    c = ctx % 2
    row = ctx // 2
    unit = ctx * 4 + x
    par = x % 2
    half = x // 2
    member = 2 * c + par
    zp = (z + par + 1) % 2
    base = 8 * row + x - 8
    sibling = (ctx - c + (1 - c), x)

    def dev(v):
        return (v // 4, v % 4)

    def remote(src, dst, send, recv, device):
        return pltpu.make_async_remote_copy(
            src_ref=src, dst_ref=dst, send_sem=send, recv_sem=recv, device_id=device, device_id_type=MESH)

    barrier = pltpu.get_barrier_semaphore()

    def greet(device):
        pl.semaphore_signal(barrier, inc=1, device_id=device, device_id_type=MESH)

    def later(act):
        loop(0, (16 - z - par) // 2, lambda i: act(z + 2 * i + 2 - (1 - par)))

    def earlier(act):
        loop(0, (z + 1 - par) // 2, lambda i: act(z - 2 * i - 2 + (1 - par)))

    earlier(lambda zz: greet((zz * 8 + y * 2 + c, x)))

    def run_before(k):
        return 8 * row + 4 * k + 2 * half - 1

    for k in range(2):
        @pl.when(run_before(k) >= 0)
        def _():
            greet(dev(run_before(k)))

    for m in range(1, 4):
        greet((ctx - c + (c + m // 2) % 2, x - par + (par + m % 2) % 2))
        greet((ctx, (x + m) % 4))
        greet((z * 8 + ((y + m) % 4) * 2 + c, x))
    greet(sibling)

    def source_slots(act):
        def one(s):
            @pl.when(jnp.logical_and(base + s >= 0, s != 8 + 4 * c))
            def _():
                act(s)

        loop(0, 13, one)

    def greet_source(s):
        v = base + s
        passed = jnp.logical_and(v < 8 * row, v % 4 != x)
        greet((jnp.where(passed, ctx, v // 4), v % 4))

    source_slots(greet_source)

    for h in range(2):
        own[h, :, 0:384] = kr[:, 384 * h:384 * h + 384]
        own[h, :, 384:640] = vr[:, 256 * h:256 * h + 256]
        mix[h, :, 0:192] = kmix[2 * h].astype(F32)
        mix[h, :, 192:384] = kmix[2 * h + 1].astype(F32)
        mix[h, :, 384:512] = vmix[2 * h].astype(F32)
        mix[h, :, 512:640] = vmix[2 * h + 1].astype(F32)
        kp[h] = jnp.zeros((384, 384), BF)
        kp[h, 0:192, 0:192] = kproj[2 * h]
        kp[h, 192:384, 192:384] = kproj[2 * h + 1]

    rows16 = lax.broadcasted_iota(jnp.int32, (16, 1), 0)
    crosses = jnp.logical_and(par == 1, unit < UNITS - 1)
    for h in range(2):
        rows = own[h].astype(F32).reshape(4, 16, 640)
        begins = jnp.sum(rows * mix[h, 0:16][None], axis=1)
        ends = jnp.sum(rows * mix[h, 16:32][None], axis=1)
        shares = jnp.concatenate([ends[0:1], ends[1:4] + begins[0:3]], 0)
        placed = jnp.where(rows16 // 4 == member, jnp.concatenate([shares] * 4, 0), 0.0)
        within = jnp.logical_and(rows16 == 4 * (member + 1), par == 0)
        tile[h] = placed + jnp.where(within, begins[3:4], 0.0)
        tail[h] = jnp.where(rows16[0:8] == 0, begins[3:4], 0.0)

    next_row = (row < 63).astype(jnp.int32)
    targets = jnp.where(c == 0, 7, 2 * (3 - x) + 1) + 2 * next_row + jnp.where(row > 0, x + 3, 0)
    pl.semaphore_wait(
        barrier,
        targets + 4 * crosses.astype(jnp.int32) + 10 + (16 - z - par) // 2)

    def quad_copy(m_to, m_from, device):
        return remote(tile.at[m_to // 2], quad.at[m_from], quad_s.at[m_to], quad_r.at[m_from], device)

    for m in range(4):
        @pl.when(m != member)
        def _():
            quad_copy(m, member, (ctx - c + m // 2, x - par + m % 2)).start()

    follower = unit + 1
    run = (follower % 8) // 4

    def tail_copy(h, p):
        device = (2 * (follower // 8) + h, 2 * ((follower % 4) // 2) + p)
        return remote(tail.at[h], tail_in.at[run], tail_s.at[h, p], tail_r.at[run], device)

    def tails(act):
        @pl.when(crosses)
        def _():
            for h in range(2):
                for p in range(2):
                    act(tail_copy(h, p))

    tails(lambda copy: copy.start())

    def win_copy(h, nxt, x_to, slot, device):
        return remote(own.at[h], win.at[h, slot], win_s.at[h, nxt, x_to], win_r.at[slot], device)

    def win_targets(act):
        for nxt in range(2):
            for m in range(4 - 3 * nxt):
                x_to = (x + m) % 4
                slot = unit - (8 * (row + nxt) + x_to - 8)
                needed = jnp.logical_and(slot >= 0, slot <= 12)
                needed = jnp.logical_and(needed, row + nxt < 64)
                for h in range(2):
                    ctx_to = 2 * (row + nxt) + h
                    other = jnp.logical_or(ctx_to != ctx, x_to != x)

                    @pl.when(jnp.logical_and(needed, other))
                    def _():
                        act(win_copy(h, nxt, x_to, slot, (ctx_to, x_to)))

    win_targets(lambda copy: copy.start())
    own_copy = pltpu.make_async_copy(own.at[c], win.at[c, 8 + 4 * c], own_sem)
    own_copy.start()

    @pl.when(row == 0)
    def _():
        def clear(s):
            win[c, s] = jnp.zeros((64, 640), BF)

        loop(0, 8 - x, clear)

    def clear_plane(zz):
        @pl.when(zz % 2 == zp)
        def _():
            comp[c, zz // 2, zz % 2, y, half] = jnp.zeros((16, 640), BF)

    loop(z + 1, 4 * (z // 4) + 4, clear_plane)

    @pl.when((z // 4) % 2 == 0)
    def _():
        def clear(i):
            comp[:, 2 * (z // 4) + 2 + i] = jnp.zeros((2, 2, 4, 2, 16, 640), BF)

        loop(0, 2, clear)

    total = tile[c]
    for m in range(4):
        @pl.when(m != member)
        def _():
            quad_copy(m, m, (ctx, x)).wait_recv()
    for k in range(2):
        @pl.when(run_before(k) >= 0)
        def _():
            remote(tail.at[0], tail_in.at[k], tail_s.at[0, 0], tail_r.at[k], sibling).wait_recv()

        @pl.when(run_before(k) < 0)
        def _():
            tail_in[k] = jnp.zeros((8, 640), F32)

    for m in range(4):
        total = total + jnp.where(m == member, 0.0, quad[m])
    total = total + jnp.concatenate([tail_in[0], tail_in[1]], 0)
    pooled = total.astype(BF)
    keys = jnp.dot(pooled[:, 0:384], kp[c], preferred_element_type=F32)
    v0 = jnp.dot(pooled[:, 384:512], vproj[2 * c], preferred_element_type=F32)
    v1 = jnp.dot(pooled[:, 512:640], vproj[2 * c + 1], preferred_element_type=F32)
    no_block = jnp.logical_and(jnp.logical_and(row == 0, half == 0), rows16 == 0)
    piece[:, 0:384] = jnp.where(no_block, keys[1:2], keys).astype(BF)
    piece[:, 384:512] = jnp.where(no_block, 0.0, v0).astype(BF)
    piece[:, 512:640] = jnp.where(no_block, 0.0, v1).astype(BF)

    @pl.when(par == 1)
    def _():
        comp[c, z // 2, z % 2, y, half] = piece[...]

    def z_copy(z_from, z_to):
        ref = comp.at[c, z_from // 2, z_from % 2, y, half]
        return remote(piece, ref, z_s.at[z_to], z_r.at[z_from], (z_to * 8 + y * 2 + c, x))

    later(lambda zz: z_copy(z, zz).start())

    lane = lax.broadcasted_iota(jnp.int32, (64, 256), 1)
    zero = jnp.zeros((64, 256), F32)
    q_copy.wait()
    for head in range(64):
        g, hh = head // 16, head % 16
        at = 384 * (head // 2) + 128 * (head % 2)
        t = q_ref[:, at:at + 256].astype(F32)
        if head % 2 != g % 2:
            t = pltpu.roll(t, 192 if head % 2 else 64, 1)
        t = jnp.where(lane < 192 if g % 2 == 0 else lane >= 64, t, zero)
        qs[g, 64 * hh:64 * hh + 64, :] = t.astype(BF)
    sig = jax.nn.sigmoid(gates[...].astype(F32))
    for head in range(64):
        g, hh = head // 16, head % 16
        gc[g, 64 * hh:64 * hh + 64, :] = jnp.broadcast_to(sig[:, 2 * head:2 * head + 1], (64, 128))
        gw[g, 64 * hh:64 * hh + 64, :] = jnp.broadcast_to(sig[:, 2 * head + 1:2 * head + 2], (64, 128))
    vx[:, :, 128:256] = jnp.ones((4, KC, 128), BF)

    i = lax.broadcasted_iota(jnp.int32, (64, WK), 0)
    k = lax.broadcasted_iota(jnp.int32, (64, WK), 1)
    bw[...] = jnp.where((k > i) & (k <= i + 512) & (k + 64 * (unit - 8) >= 0), 0.0, NEG)
    last_chunk = z // 8
    i = lax.broadcasted_iota(jnp.int32, (64, KC), 0)
    k = lax.broadcasted_iota(jnp.int32, (64, KC), 1)
    r = k % 128
    m = (r % 16) // 4
    u = 8 * (4 * (8 * last_chunk + k // 128) + r // 32) + 4 * (m // 2) + 2 * ((r % 32) // 16) + m % 2
    b = 4 * u - 1 + r % 4
    bc[...] = jnp.where((16 * b + 31 <= 64 * unit + i) & (b >= 0), 0.0, NEG)

    def pass_copy(k, m):
        x_to = (x + m) % 4
        return remote(
            win.at[c, 4 * k], win.at[c, 4 * k + x - x_to], pass_s.at[k, m], win_r.at[4 * k + x - x_to], (ctx, x_to))

    def passes(k, act):
        for m in (1, 3, 2):
            @pl.when(jnp.logical_or(k == 1, (x + m) % 4 < x))
            def _():
                act(pass_copy(k, m))

    def win_wait(s):
        remote(own.at[0], win.at[c, s], win_s.at[0, 0, 0], win_r.at[s], sibling).wait_recv()

    @pl.when(row > 0)
    def _():
        for k in (1, 0):
            win_wait(4 * k)
            passes(k, lambda copy: copy.start())

    earlier(lambda zz: z_copy(zz, z).wait_recv())

    def peer(along_x, d):
        if along_x:
            return (ctx, (x + d) % 4)
        return (z * 8 + ((y + d) % 4) * 2 + c, x)

    def a_copy(ci, d, xx, yy):
        pp = (z + xx % 2 + 1) % 2
        ref = comp.at[c, pl.ds(2 * ci, 2), pp, yy, xx // 2]
        return remote(ref, ref, a_s.at[ci, d - 1], a_r.at[ci, d - 1], peer(ci % 2 == 0, d))

    def b_copy(ci, d, xx, yy):
        if ci % 2 == 0:
            ref = comp.at[c, pl.ds(2 * ci, 2), :, yy]
        else:
            ref = comp.at[c, pl.ds(2 * ci, 2), (z + xx % 2 + 1) % 2, :, xx // 2]
        return remote(ref, ref, b_s.at[ci, d - 1], b_r.at[ci, d - 1], peer(ci % 2 == 1, d))

    def d_copy(ci, cc):
        ref = comp.at[cc, pl.ds(2 * ci, 2)]
        return remote(ref, ref, d_s.at[ci], d_r.at[ci], sibling)

    def back(along_x, d):
        return ((x + 4 - d) % 4, y) if along_x else (x, (y + 4 - d) % 4)

    def chunks(which, act):
        for ci in which:
            @pl.when(4 * ci <= z)
            def _():
                act(ci)

    def send_a(ci):
        for d in (1, 3, 2):
            a_copy(ci, d, x, y).start()

    def send_b(ci):
        for d in (1, 3, 2):
            a_copy(ci, d, *back(ci % 2 == 0, d)).wait_recv()
        for d in (1, 3, 2):
            b_copy(ci, d, x, y).start()

    def send_d(ci):
        for d in (1, 3, 2):
            b_copy(ci, d, *back(ci % 2 == 1, d)).wait_recv()
        d_copy(ci, c).start()

    chunks((3, 2, 1, 0), send_a)

    def win_rest(s):
        @pl.when(jnp.logical_and(s != 0, s != 4))
        def _():
            win_wait(s)

    source_slots(win_rest)
    own_copy.wait()

    def relay(cc, first):
        ref = win.at[cc, pl.ds(4 * first, 9)]
        return remote(ref, ref, rel_s, rel_r, sibling)

    relay(c, 1 - c).start()

    def scores(g, tile, keys):
        q = qs[g, pl.ds(pl.multiple_of(tile * RT, RT), RT), :]
        return lax.dot_general(q, keys, (((1,), (1,)), ((), ())), preferred_element_type=F32)

    def biased(s, bias):
        width = s.shape[1]
        return (s.reshape(RT // 64, 64, width) + bias[...][None]).reshape(RT, width)

    def win_keys(h, odd):
        return win[h, pl.ds(4 * c, 9), :, 128 * odd:128 * odd + 256].reshape(WK, 256)

    def win_done(s, g, tile):
        rows = pl.ds(pl.multiple_of(tile * RT, RT), RT)
        s = biased(s, bw)
        top = jnp.max(s, axis=1, keepdims=True)
        p = jnp.exp((s - top) * SCALE).astype(BF)
        a = jnp.dot(p, vx[g, 0:WK, :], preferred_element_type=F32)
        owin[g, rows, :] = gw[g, rows, :] * a[:, 0:128] / a[:, 128:256]

    def comp_keys(h, odd, chunk):
        return comp[h, pl.ds(4 * chunk, 4), :, :, :, :, 128 * odd:128 * odd + 256].reshape(KC, 256)

    def comp_done(s, g, tile, first):
        rows = pl.ds(pl.multiple_of(tile * RT, RT), RT)
        if first:
            s = biased(s, bc)
            top = jnp.maximum(jnp.max(s, axis=1, keepdims=True), FLOOR)
            p = jnp.exp((s - top) * SCALE).astype(BF)
            acc[g, rows, :] = jnp.dot(p, vx[g], preferred_element_type=F32)
        else:
            before = mx[g, rows, 0:1]
            top = jnp.maximum(jnp.max(s, axis=1, keepdims=True), before)
            p = jnp.exp((s - top) * SCALE).astype(BF)
            factor = jnp.exp((before - top) * SCALE)
            acc[g, rows, :] = acc[g, rows, :] * factor + jnp.dot(p, vx[g], preferred_element_type=F32)
        mx[g, rows, :] = jnp.broadcast_to(top, (RT, 128))

    tiles = 1024 // RT

    def run_half(h, width, keys, done):
        s0[:, 0:width] = scores(2 * h, 0, keys(h, 0))

        def body(t):
            s1[:, 0:width] = scores(2 * h + 1, t, keys(h, 1))
            done(s0[:, 0:width], 2 * h, t)
            s0[:, 0:width] = scores(2 * h, jnp.minimum(t + 1, tiles - 1), keys(h, 0))
            done(s1[:, 0:width], 2 * h + 1, t)

        loop(0, tiles, body)

    def win_half(h):
        for odd in range(2):
            at = 384 + 128 * odd
            vx[2 * h + odd, 0:WK, 0:128] = win[h, pl.ds(4 * c, 9), :, at:at + 128].reshape(WK, 128)
        run_half(h, WK, win_keys, win_done)

    def comp_half(h, chunk, first):
        for odd in range(2):
            at = 384 + 128 * odd
            vx[2 * h + odd, :, 0:128] = comp[h, pl.ds(4 * chunk, 4), :, :, :, :, at:at + 128].reshape(KC, 128)
        weight = jnp.where(jnp.logical_and(chunk == 0, rows16 == 0), 0.0, 1.0).astype(BF)
        for odd in range(2):
            vx[2 * h + odd, 0:16, 128:256] = jnp.broadcast_to(weight, (16, 128))
        run_half(h, KC, lambda hh, odd: comp_keys(hh, odd, chunk),
                 lambda s, g, t: comp_done(s, g, t, first))

    def nearest(act):
        @pl.when(z >= 8)
        def _():
            chunks((3, 2), act)

        @pl.when(z < 8)
        def _():
            chunks((1, 0), act)

    def farther(act):
        @pl.when(z >= 8)
        def _():
            chunks((1, 0), act)

    def wait_d(ci):
        d_copy(ci, 1 - c).wait_recv()

    win_half(c)
    nearest(send_b)
    relay(1 - c, c).wait_recv()
    win_half(1 - c)
    nearest(send_d)
    farther(send_b)
    comp_half(c, last_chunk, True)
    nearest(wait_d)
    comp_half(1 - c, last_chunk, True)
    farther(send_d)

    @pl.when(z >= 8)
    def _():
        comp_half(c, jnp.int32(0), False)

    farther(wait_d)

    @pl.when(z >= 8)
    def _():
        comp_half(1 - c, jnp.int32(0), False)

    for g in range(4):
        for hh in range(16):
            rows = slice(64 * hh, 64 * hh + 64)
            weight = acc[g, rows, 128:256]
            o = gc[g, rows, :] * acc[g, rows, 0:128] / jnp.where(weight > 0.0, weight, 1.0) + owin[g, rows, :]
            at = 128 * (16 * g + hh)
            out[:, at:at + 128] = o.astype(BF)

    def sent(ci):
        d_copy(ci, c).wait_send()
        for d in (1, 2, 3):
            a_copy(ci, d, x, y).wait_send()
            b_copy(ci, d, x, y).wait_send()

    chunks((3, 2, 1, 0), sent)
    relay(c, 1 - c).wait_send()
    win_targets(lambda copy: copy.wait_send())

    @pl.when(row > 0)
    def _():
        for k in (1, 0):
            passes(k, lambda copy: copy.wait_send())

    later(lambda zz: z_copy(z, zz).wait_send())
    for m in range(4):
        @pl.when(m != member)
        def _():
            quad_copy(m, member, (ctx, x)).wait_send()

    tails(lambda copy: copy.wait_send())


def local(queries, key_rows, values, gate_logits, key_mix, key_proj, value_mix, value_proj):
    dma = pltpu.SemaphoreType.DMA
    vmem = pl.BlockSpec(memory_space=pltpu.VMEM)
    return pl.pallas_call(
        fused_kernel,
        out_shape=jax.ShapeDtypeStruct((64, 8192), BF),
        in_specs=[pl.BlockSpec(memory_space=pl.ANY)] + [vmem] * 7,
        out_specs=vmem,
        scratch_shapes=[
            pltpu.VMEM((64, 12288), BF),
            pltpu.VMEM((2, 64, 640), BF),
            pltpu.VMEM((2, 32, 640), F32),
            pltpu.VMEM((2, 384, 384), BF),
            pltpu.VMEM((2, 16, 640), F32),
            pltpu.VMEM((2, 8, 640), F32),
            pltpu.VMEM((4, 16, 640), F32),
            pltpu.VMEM((2, 8, 640), F32),
            pltpu.VMEM((16, 640), BF),
            pltpu.VMEM((2, 13, 64, 640), BF),
            pltpu.VMEM((2, 8, 2, 4, 2, 16, 640), BF),
            pltpu.VMEM((4, 1024, 256), BF),
            pltpu.VMEM((4, 1024, 128), F32),
            pltpu.VMEM((4, 1024, 128), F32),
            pltpu.VMEM((4, KC, 256), BF),
            pltpu.VMEM((4, 1024, 256), F32),
            pltpu.VMEM((4, 1024, 128), F32),
            pltpu.VMEM((4, 1024, 128), F32),
            pltpu.VMEM((RT, KC), F32),
            pltpu.VMEM((RT, KC), F32),
            pltpu.VMEM((64, WK), F32),
            pltpu.VMEM((64, KC), F32),
            dma, dma((2, 2)), dma((2,)), dma((2, 2, 4)), dma((13,)), dma, dma, dma, dma((4,)), dma((4,)), dma((16,)), dma((16,)),
            dma((4, 3)), dma((4, 3)), dma((4, 3)), dma((4, 3)), dma((4,)), dma((4,)), dma((2, 4)),
        ],
        compiler_params=pltpu.CompilerParams(
            collective_id=0, has_side_effects=True, vmem_limit_bytes=56 * 2**20),
        cost_estimate=pl.CostEstimate(flops=10**10, bytes_accessed=10**7, transcendentals=10**7),
    )(queries, key_rows, values, gate_logits, key_mix, key_proj, value_mix, value_proj)


def solution(mesh):
    rows = P(("ctx", "head"), None)
    return jax.shard_map(
        local, mesh=mesh, in_specs=(rows,) * 4 + (P(),) * 4, out_specs=rows, check_vma=False)
```

```python
import math

import jax
import jax.numpy as jnp
from jax import lax
from jax.experimental import pallas as pl
from jax.experimental.pallas import tpu as pltpu
from jax.sharding import PartitionSpec as P

BF = jnp.bfloat16
F32 = jnp.float32
MESH = pl.DeviceIdType.MESH
UNITS = 512
SCALE = 1.0 / math.sqrt(192.0)
NEG = -1e30
FLOOR = -1e29
RT = 512
KC = 1024
WK = 576


def loop(lower, upper, act):
    def body(i, carry):
        act(i)
        return carry

    lax.fori_loop(lower, upper, body, 0)


def fused_kernel(
    q_any, kr, vr, gates, kmix, kproj, vmix, vproj,
    out,
    q_ref, own, mix, kp, tile, tail, quad, tail_in, piece, win, comp, qs, gw, gc, vx, acc, mx, owin, s0, s1, bw, bc,
    q_sem, tail_s, tail_r, win_s, win_r, own_sem, rel_s, rel_r, quad_s, quad_r, z_s, z_r,
    a_s, a_r, b_s, b_r, d_s, d_r, pass_s,
):
    q_copy = pltpu.make_async_copy(q_any, q_ref, q_sem)
    q_copy.start()
    ctx = lax.axis_index("ctx")
    x = lax.axis_index("head")
    z = ctx // 8
    y = (ctx // 2) % 4
    c = ctx % 2
    row = ctx // 2
    unit = ctx * 4 + x
    par = x % 2
    half = x // 2
    member = 2 * c + par
    zp = (z + par + 1) % 2
    base = 8 * row + x - 8
    sibling = (ctx - c + (1 - c), x)

    def dev(v):
        return (v // 4, v % 4)

    def remote(src, dst, send, recv, device):
        return pltpu.make_async_remote_copy(
            src_ref=src, dst_ref=dst, send_sem=send, recv_sem=recv, device_id=device, device_id_type=MESH)

    barrier = pltpu.get_barrier_semaphore()

    def greet(device):
        pl.semaphore_signal(barrier, inc=1, device_id=device, device_id_type=MESH)

    def later(act):
        loop(0, (16 - z - par) // 2, lambda i: act(z + 2 * i + 2 - (1 - par)))

    def earlier(act):
        loop(0, (z + 1 - par) // 2, lambda i: act(z - 2 * i - 2 + (1 - par)))

    def await_planes(lower, upper):
        loop(lower, upper, lambda i: z_copy(z - 2 * i - 2 + (1 - par), z).wait_recv())

    near_planes = (z % 8 + 1 - par) // 2

    earlier(lambda zz: greet((zz * 8 + y * 2 + c, x)))

    def run_before(k):
        return 8 * row + 4 * k + 2 * half - 1

    for k in range(2):
        @pl.when(run_before(k) >= 0)
        def _():
            greet(dev(run_before(k)))

    for m in range(1, 4):
        greet((ctx - c + (c + m // 2) % 2, x - par + (par + m % 2) % 2))
        greet((ctx, (x + m) % 4))
        greet((z * 8 + ((y + m) % 4) * 2 + c, x))
    greet(sibling)

    def source_slots(act):
        def one(s):
            @pl.when(jnp.logical_and(base + s >= 0, s != 8 + 4 * c))
            def _():
                act(s)

        loop(0, 13, one)

    def greet_source(s):
        v = base + s
        passed = jnp.logical_and(v < 8 * row, v % 4 != x)
        greet((jnp.where(passed, ctx, v // 4), v % 4))

    source_slots(greet_source)

    for h in range(2):
        own[h, :, 0:384] = kr[:, 384 * h:384 * h + 384]
        own[h, :, 384:640] = vr[:, 256 * h:256 * h + 256]
        mix[h, :, 0:192] = kmix[2 * h].astype(F32)
        mix[h, :, 192:384] = kmix[2 * h + 1].astype(F32)
        mix[h, :, 384:512] = vmix[2 * h].astype(F32)
        mix[h, :, 512:640] = vmix[2 * h + 1].astype(F32)
        kp[h] = jnp.zeros((384, 384), BF)
        kp[h, 0:192, 0:192] = kproj[2 * h]
        kp[h, 192:384, 192:384] = kproj[2 * h + 1]

    rows16 = lax.broadcasted_iota(jnp.int32, (16, 1), 0)
    crosses = jnp.logical_and(par == 1, unit < UNITS - 1)
    for h in range(2):
        rows = own[h].astype(F32).reshape(4, 16, 640)
        begins = jnp.sum(rows * mix[h, 0:16][None], axis=1)
        ends = jnp.sum(rows * mix[h, 16:32][None], axis=1)
        shares = jnp.concatenate([ends[0:1], ends[1:4] + begins[0:3]], 0)
        placed = jnp.where(rows16 // 4 == member, jnp.concatenate([shares] * 4, 0), 0.0)
        within = jnp.logical_and(rows16 == 4 * (member + 1), par == 0)
        tile[h] = placed + jnp.where(within, begins[3:4], 0.0)
        tail[h] = jnp.where(rows16[0:8] == 0, begins[3:4], 0.0)

    next_row = (row < 63).astype(jnp.int32)
    targets = jnp.where(c == 0, 7, 2 * (3 - x) + 1) + 2 * next_row + jnp.where(row > 0, x + 3, 0)
    pl.semaphore_wait(
        barrier,
        targets + 4 * crosses.astype(jnp.int32) + 10 + (16 - z - par) // 2)

    def quad_copy(m_to, m_from, device):
        return remote(tile.at[m_to // 2], quad.at[m_from], quad_s.at[m_to], quad_r.at[m_from], device)

    for m in range(4):
        @pl.when(m != member)
        def _():
            quad_copy(m, member, (ctx - c + m // 2, x - par + m % 2)).start()

    follower = unit + 1
    run = (follower % 8) // 4

    def tail_copy(h, p):
        device = (2 * (follower // 8) + h, 2 * ((follower % 4) // 2) + p)
        return remote(tail.at[h], tail_in.at[run], tail_s.at[h, p], tail_r.at[run], device)

    def tails(act):
        @pl.when(crosses)
        def _():
            for h in range(2):
                for p in range(2):
                    act(tail_copy(h, p))

    tails(lambda copy: copy.start())

    def win_copy(h, nxt, x_to, slot, device):
        return remote(own.at[h], win.at[h, slot], win_s.at[h, nxt, x_to], win_r.at[slot], device)

    def win_targets(act):
        for nxt in (1, 0):
            for m in range(4 - 3 * nxt):
                x_to = (x + m) % 4
                slot = unit - (8 * (row + nxt) + x_to - 8)
                needed = jnp.logical_and(slot >= 0, slot <= 12)
                needed = jnp.logical_and(needed, row + nxt < 64)
                for h in range(2):
                    ctx_to = 2 * (row + nxt) + h
                    other = jnp.logical_or(ctx_to != ctx, x_to != x)

                    @pl.when(jnp.logical_and(needed, other))
                    def _():
                        act(win_copy(h, nxt, x_to, slot, (ctx_to, x_to)))

    win_targets(lambda copy: copy.start())
    own_copy = pltpu.make_async_copy(own.at[c], win.at[c, 8 + 4 * c], own_sem)
    own_copy.start()

    @pl.when(row == 0)
    def _():
        def clear(s):
            win[c, s] = jnp.zeros((64, 640), BF)

        loop(0, 8 - x, clear)

    def clear_plane(zz):
        @pl.when(zz % 2 == zp)
        def _():
            comp[c, zz // 2, zz % 2, y, half] = jnp.zeros((16, 640), BF)

    loop(z + 1, 4 * (z // 4) + 4, clear_plane)

    @pl.when((z // 4) % 2 == 0)
    def _():
        def clear(i):
            comp[:, 2 * (z // 4) + 2 + i] = jnp.zeros((2, 2, 4, 2, 16, 640), BF)

        loop(0, 2, clear)

    total = tile[c]
    for m in range(4):
        @pl.when(m != member)
        def _():
            quad_copy(m, m, (ctx, x)).wait_recv()
    for k in range(2):
        @pl.when(run_before(k) >= 0)
        def _():
            remote(tail.at[0], tail_in.at[k], tail_s.at[0, 0], tail_r.at[k], sibling).wait_recv()

        @pl.when(run_before(k) < 0)
        def _():
            tail_in[k] = jnp.zeros((8, 640), F32)

    for m in range(4):
        total = total + jnp.where(m == member, 0.0, quad[m])
    total = total + jnp.concatenate([tail_in[0], tail_in[1]], 0)
    pooled = total.astype(BF)
    keys = jnp.dot(pooled[:, 0:384], kp[c], preferred_element_type=F32)
    v0 = jnp.dot(pooled[:, 384:512], vproj[2 * c], preferred_element_type=F32)
    v1 = jnp.dot(pooled[:, 512:640], vproj[2 * c + 1], preferred_element_type=F32)
    no_block = jnp.logical_and(jnp.logical_and(row == 0, half == 0), rows16 == 0)
    piece[:, 0:384] = jnp.where(no_block, keys[1:2], keys).astype(BF)
    piece[:, 384:512] = jnp.where(no_block, 0.0, v0).astype(BF)
    piece[:, 512:640] = jnp.where(no_block, 0.0, v1).astype(BF)

    @pl.when(par == 1)
    def _():
        comp[c, z // 2, z % 2, y, half] = piece[...]

    def z_copy(z_from, z_to):
        ref = comp.at[c, z_from // 2, z_from % 2, y, half]
        return remote(piece, ref, z_s.at[z_to], z_r.at[z_from], (z_to * 8 + y * 2 + c, x))

    later(lambda zz: z_copy(z, zz).start())

    lane = lax.broadcasted_iota(jnp.int32, (64, 256), 1)
    zero = jnp.zeros((64, 256), F32)
    q_copy.wait()
    for head in range(64):
        g, hh = head // 16, head % 16
        at = 384 * (head // 2) + 128 * (head % 2)
        t = q_ref[:, at:at + 256].astype(F32)
        if head % 2 != g % 2:
            t = pltpu.roll(t, 192 if head % 2 else 64, 1)
        t = jnp.where(lane < 192 if g % 2 == 0 else lane >= 64, t, zero)
        qs[g, 64 * hh:64 * hh + 64, :] = t.astype(BF)
    sig = jax.nn.sigmoid(gates[...].astype(F32))
    for head in range(64):
        g, hh = head // 16, head % 16
        gc[g, 64 * hh:64 * hh + 64, :] = jnp.broadcast_to(sig[:, 2 * head:2 * head + 1], (64, 128))
        gw[g, 64 * hh:64 * hh + 64, :] = jnp.broadcast_to(sig[:, 2 * head + 1:2 * head + 2], (64, 128))
    vx[:, :, 128:256] = jnp.ones((4, KC, 128), BF)

    i = lax.broadcasted_iota(jnp.int32, (64, WK), 0)
    k = lax.broadcasted_iota(jnp.int32, (64, WK), 1)
    bw[...] = jnp.where((k > i) & (k <= i + 512) & (k + 64 * (unit - 8) >= 0), 0.0, NEG)
    last_chunk = z // 8
    i = lax.broadcasted_iota(jnp.int32, (64, KC), 0)
    k = lax.broadcasted_iota(jnp.int32, (64, KC), 1)
    r = k % 128
    m = (r % 16) // 4
    u = 8 * (4 * (8 * last_chunk + k // 128) + r // 32) + 4 * (m // 2) + 2 * ((r % 32) // 16) + m % 2
    b = 4 * u - 1 + r % 4
    bc[...] = jnp.where((16 * b + 31 <= 64 * unit + i) & (b >= 0), 0.0, NEG)

    def pass_copy(k, m):
        x_to = (x + m) % 4
        return remote(
            win.at[c, 4 * k], win.at[c, 4 * k + x - x_to], pass_s.at[k, m], win_r.at[4 * k + x - x_to], (ctx, x_to))

    def passes(k, act):
        for m in (1, 3, 2):
            @pl.when(jnp.logical_or(k == 1, (x + m) % 4 < x))
            def _():
                act(pass_copy(k, m))

    def win_wait(s):
        remote(own.at[0], win.at[c, s], win_s.at[0, 0, 0], win_r.at[s], sibling).wait_recv()

    @pl.when(row > 0)
    def _():
        for k in (1, 0):
            win_wait(4 * k)
            passes(k, lambda copy: copy.start())

    await_planes(0, near_planes)

    def peer(along_x, d):
        if along_x:
            return (ctx, (x + d) % 4)
        return (z * 8 + ((y + d) % 4) * 2 + c, x)

    def a_copy(ci, d, xx, yy):
        pp = (z + xx % 2 + 1) % 2
        ref = comp.at[c, pl.ds(2 * ci, 2), pp, yy, xx // 2]
        return remote(ref, ref, a_s.at[ci, d - 1], a_r.at[ci, d - 1], peer(ci % 2 == 0, d))

    def b_copy(ci, d, xx, yy):
        if ci % 2 == 0:
            ref = comp.at[c, pl.ds(2 * ci, 2), :, yy]
        else:
            ref = comp.at[c, pl.ds(2 * ci, 2), (z + xx % 2 + 1) % 2, :, xx // 2]
        return remote(ref, ref, b_s.at[ci, d - 1], b_r.at[ci, d - 1], peer(ci % 2 == 1, d))

    def d_copy(ci, cc):
        ref = comp.at[cc, pl.ds(2 * ci, 2)]
        return remote(ref, ref, d_s.at[ci], d_r.at[ci], sibling)

    def back(along_x, d):
        return ((x + 4 - d) % 4, y) if along_x else (x, (y + 4 - d) % 4)

    def chunks(which, act):
        for ci in which:
            @pl.when(4 * ci <= z)
            def _():
                act(ci)

    def send_a(ci):
        for d in (1, 3, 2):
            a_copy(ci, d, x, y).start()

    def send_b(ci):
        for d in (1, 3, 2):
            a_copy(ci, d, *back(ci % 2 == 0, d)).wait_recv()
        for d in (1, 3, 2):
            b_copy(ci, d, x, y).start()

    def send_d(ci):
        for d in (1, 3, 2):
            b_copy(ci, d, *back(ci % 2 == 1, d)).wait_recv()
        d_copy(ci, c).start()

    @pl.when(z >= 8)
    def _():
        chunks((3, 2), send_a)

    @pl.when(z < 8)
    def _():
        chunks((1, 0), send_a)

    def win_rest(s):
        @pl.when(jnp.logical_and(s != 0, s != 4))
        def _():
            win_wait(s)

    source_slots(win_rest)
    own_copy.wait()

    def relay(cc, first):
        ref = win.at[cc, pl.ds(4 * first, 9)]
        return remote(ref, ref, rel_s, rel_r, sibling)

    relay(c, 1 - c).start()

    def scores(g, tile, keys):
        q = qs[g, pl.ds(pl.multiple_of(tile * RT, RT), RT), :]
        return lax.dot_general(q, keys, (((1,), (1,)), ((), ())), preferred_element_type=F32)

    def biased(s, bias):
        width = s.shape[1]
        return (s.reshape(RT // 64, 64, width) + bias[...][None]).reshape(RT, width)

    def win_keys(h, odd):
        return win[h, pl.ds(4 * c, 9), :, 128 * odd:128 * odd + 256].reshape(WK, 256)

    def win_done(s, g, tile):
        rows = pl.ds(pl.multiple_of(tile * RT, RT), RT)
        s = biased(s, bw)
        top = jnp.max(s, axis=1, keepdims=True)
        p = jnp.exp((s - top) * SCALE).astype(BF)
        a = jnp.dot(p, vx[g, 0:WK, :], preferred_element_type=F32)
        owin[g, rows, :] = gw[g, rows, :] * a[:, 0:128] / a[:, 128:256]

    def comp_keys(h, odd, chunk):
        return comp[h, pl.ds(4 * chunk, 4), :, :, :, :, 128 * odd:128 * odd + 256].reshape(KC, 256)

    def comp_done(s, g, tile, first):
        rows = pl.ds(pl.multiple_of(tile * RT, RT), RT)
        if first:
            s = biased(s, bc)
            top = jnp.maximum(jnp.max(s, axis=1, keepdims=True), FLOOR)
            p = jnp.exp((s - top) * SCALE).astype(BF)
            acc[g, rows, :] = jnp.dot(p, vx[g], preferred_element_type=F32)
        else:
            before = mx[g, rows, 0:1]
            top = jnp.maximum(jnp.max(s, axis=1, keepdims=True), before)
            p = jnp.exp((s - top) * SCALE).astype(BF)
            factor = jnp.exp((before - top) * SCALE)
            acc[g, rows, :] = acc[g, rows, :] * factor + jnp.dot(p, vx[g], preferred_element_type=F32)
        mx[g, rows, :] = jnp.broadcast_to(top, (RT, 128))

    tiles = 1024 // RT

    def run_half(h, width, keys, done):
        s0[:, 0:width] = scores(2 * h, 0, keys(h, 0))

        def body(t):
            s1[:, 0:width] = scores(2 * h + 1, t, keys(h, 1))
            done(s0[:, 0:width], 2 * h, t)
            s0[:, 0:width] = scores(2 * h, jnp.minimum(t + 1, tiles - 1), keys(h, 0))
            done(s1[:, 0:width], 2 * h + 1, t)

        loop(0, tiles, body)

    def win_half(h):
        for odd in range(2):
            at = 384 + 128 * odd
            vx[2 * h + odd, 0:WK, 0:128] = win[h, pl.ds(4 * c, 9), :, at:at + 128].reshape(WK, 128)
        run_half(h, WK, win_keys, win_done)

    def comp_half(h, chunk, first):
        for odd in range(2):
            at = 384 + 128 * odd
            vx[2 * h + odd, :, 0:128] = comp[h, pl.ds(4 * chunk, 4), :, :, :, :, at:at + 128].reshape(KC, 128)
        weight = jnp.where(jnp.logical_and(chunk == 0, rows16 == 0), 0.0, 1.0).astype(BF)
        for odd in range(2):
            vx[2 * h + odd, 0:16, 128:256] = jnp.broadcast_to(weight, (16, 128))
        run_half(h, KC, lambda hh, odd: comp_keys(hh, odd, chunk),
                 lambda s, g, t: comp_done(s, g, t, first))

    def nearest(act):
        @pl.when(z >= 8)
        def _():
            chunks((3, 2), act)

        @pl.when(z < 8)
        def _():
            chunks((1, 0), act)

    def farther(act):
        @pl.when(z >= 8)
        def _():
            chunks((1, 0), act)

    def wait_d(ci):
        d_copy(ci, 1 - c).wait_recv()

    win_half(c)
    nearest(send_b)
    await_planes(near_planes, (z + 1 - par) // 2)
    farther(send_a)
    relay(1 - c, c).wait_recv()
    win_half(1 - c)
    nearest(send_d)
    farther(send_b)
    comp_half(c, last_chunk, True)
    nearest(wait_d)
    comp_half(1 - c, last_chunk, True)
    farther(send_d)

    @pl.when(z >= 8)
    def _():
        comp_half(c, jnp.int32(0), False)

    farther(wait_d)

    @pl.when(z >= 8)
    def _():
        comp_half(1 - c, jnp.int32(0), False)

    for g in range(4):
        for hh in range(16):
            rows = slice(64 * hh, 64 * hh + 64)
            weight = acc[g, rows, 128:256]
            o = gc[g, rows, :] * acc[g, rows, 0:128] / jnp.where(weight > 0.0, weight, 1.0) + owin[g, rows, :]
            at = 128 * (16 * g + hh)
            out[:, at:at + 128] = o.astype(BF)

    def sent(ci):
        d_copy(ci, c).wait_send()
        for d in (1, 2, 3):
            a_copy(ci, d, x, y).wait_send()
            b_copy(ci, d, x, y).wait_send()

    chunks((3, 2, 1, 0), sent)
    relay(c, 1 - c).wait_send()
    win_targets(lambda copy: copy.wait_send())

    @pl.when(row > 0)
    def _():
        for k in (1, 0):
            passes(k, lambda copy: copy.wait_send())

    later(lambda zz: z_copy(z, zz).wait_send())
    for m in range(4):
        @pl.when(m != member)
        def _():
            quad_copy(m, member, (ctx, x)).wait_send()

    tails(lambda copy: copy.wait_send())


def local(queries, key_rows, values, gate_logits, key_mix, key_proj, value_mix, value_proj):
    dma = pltpu.SemaphoreType.DMA
    vmem = pl.BlockSpec(memory_space=pltpu.VMEM)
    return pl.pallas_call(
        fused_kernel,
        out_shape=jax.ShapeDtypeStruct((64, 8192), BF),
        in_specs=[pl.BlockSpec(memory_space=pl.ANY)] + [vmem] * 7,
        out_specs=vmem,
        scratch_shapes=[
            pltpu.VMEM((64, 12288), BF),
            pltpu.VMEM((2, 64, 640), BF),
            pltpu.VMEM((2, 32, 640), F32),
            pltpu.VMEM((2, 384, 384), BF),
            pltpu.VMEM((2, 16, 640), F32),
            pltpu.VMEM((2, 8, 640), F32),
            pltpu.VMEM((4, 16, 640), F32),
            pltpu.VMEM((2, 8, 640), F32),
            pltpu.VMEM((16, 640), BF),
            pltpu.VMEM((2, 13, 64, 640), BF),
            pltpu.VMEM((2, 8, 2, 4, 2, 16, 640), BF),
            pltpu.VMEM((4, 1024, 256), BF),
            pltpu.VMEM((4, 1024, 128), F32),
            pltpu.VMEM((4, 1024, 128), F32),
            pltpu.VMEM((4, KC, 256), BF),
            pltpu.VMEM((4, 1024, 256), F32),
            pltpu.VMEM((4, 1024, 128), F32),
            pltpu.VMEM((4, 1024, 128), F32),
            pltpu.VMEM((RT, KC), F32),
            pltpu.VMEM((RT, KC), F32),
            pltpu.VMEM((64, WK), F32),
            pltpu.VMEM((64, KC), F32),
            dma, dma((2, 2)), dma((2,)), dma((2, 2, 4)), dma((13,)), dma, dma, dma, dma((4,)), dma((4,)), dma((16,)), dma((16,)),
            dma((4, 3)), dma((4, 3)), dma((4, 3)), dma((4, 3)), dma((4,)), dma((4,)), dma((2, 4)),
        ],
        compiler_params=pltpu.CompilerParams(
            collective_id=0, has_side_effects=True, vmem_limit_bytes=56 * 2**20),
        cost_estimate=pl.CostEstimate(flops=10**10, bytes_accessed=10**7, transcendentals=10**7),
    )(queries, key_rows, values, gate_logits, key_mix, key_proj, value_mix, value_proj)


def solution(mesh):
    rows = P(("ctx", "head"), None)
    return jax.shard_map(
        local, mesh=mesh, in_specs=(rows,) * 4 + (P(),) * 4, out_specs=rows, check_vma=False)
```

```python
import math

import jax
import jax.numpy as jnp
from jax import lax
from jax.experimental import pallas as pl
from jax.experimental.pallas import tpu as pltpu
from jax.sharding import PartitionSpec as P

BF = jnp.bfloat16
F32 = jnp.float32
MESH = pl.DeviceIdType.MESH
UNITS = 512
SCALE = 1.0 / math.sqrt(192.0)
NEG = -1e30
FLOOR = -1e29
RT = 512
KC = 1024
WK = 576


def loop(lower, upper, act):
    def body(i, carry):
        act(i)
        return carry

    lax.fori_loop(lower, upper, body, 0)


def fused_kernel(
    q_any, kr, vr, gates, kmix, kproj, vmix, vproj,
    out,
    q_ref, own, mix, kp, tile, tail, quad, tail_in, piece, win, comp, qs, gw, gc, vx, acc, mx, owin, s0, s1, bw, bc,
    q_sem, tail_s, tail_r, win_s, win_r, own_sem, rel_s, rel_r, quad_s, quad_r, z_s, z_r,
    a_s, a_r, b_s, b_r, d_s, d_r, pass_s,
):
    q_copy = pltpu.make_async_copy(q_any, q_ref, q_sem)
    q_copy.start()
    ctx = lax.axis_index("ctx")
    x = lax.axis_index("head")
    z = ctx // 8
    y = (ctx // 2) % 4
    c = ctx % 2
    row = ctx // 2
    unit = ctx * 4 + x
    par = x % 2
    half = x // 2
    member = 2 * c + par
    zp = (z + par + 1) % 2
    base = 8 * row + x - 8
    sibling = (ctx - c + (1 - c), x)

    def dev(v):
        return (v // 4, v % 4)

    def remote(src, dst, send, recv, device):
        return pltpu.make_async_remote_copy(
            src_ref=src, dst_ref=dst, send_sem=send, recv_sem=recv, device_id=device, device_id_type=MESH)

    barrier = pltpu.get_barrier_semaphore()

    def greet(device):
        pl.semaphore_signal(barrier, inc=1, device_id=device, device_id_type=MESH)

    def later(act):
        loop(0, (16 - z - par) // 2, lambda i: act(z + 2 * i + 2 - (1 - par)))

    def earlier(act):
        loop(0, (z + 1 - par) // 2, lambda i: act(z - 2 * i - 2 + (1 - par)))

    def await_planes(lower, upper):
        loop(lower, upper, lambda i: z_copy(z - 2 * i - 2 + (1 - par), z).wait_recv())

    near_planes = (z % 8 + 1 - par) // 2

    earlier(lambda zz: greet((zz * 8 + y * 2 + c, x)))

    def run_before(k):
        return 8 * row + 4 * k + 2 * half - 1

    for k in range(2):
        @pl.when(run_before(k) >= 0)
        def _():
            greet(dev(run_before(k)))

    for m in range(1, 4):
        greet((ctx - c + (c + m // 2) % 2, x - par + (par + m % 2) % 2))
        greet((ctx, (x + m) % 4))
        greet((z * 8 + ((y + m) % 4) * 2 + c, x))
    greet(sibling)

    def source_slots(act):
        def one(s):
            @pl.when(jnp.logical_and(base + s >= 0, s != 8 + 4 * c))
            def _():
                act(s)

        loop(0, 13, one)

    def greet_source(s):
        v = base + s
        passed = jnp.logical_and(v < 8 * row, v % 4 != x)
        greet((jnp.where(passed, ctx, v // 4), v % 4))

    source_slots(greet_source)

    for h in range(2):
        own[h, :, 0:384] = kr[:, 384 * h:384 * h + 384]
        own[h, :, 384:640] = vr[:, 256 * h:256 * h + 256]
        mix[h, :, 0:192] = kmix[2 * h].astype(F32)
        mix[h, :, 192:384] = kmix[2 * h + 1].astype(F32)
        mix[h, :, 384:512] = vmix[2 * h].astype(F32)
        mix[h, :, 512:640] = vmix[2 * h + 1].astype(F32)
        kp[h] = jnp.zeros((384, 384), BF)
        kp[h, 0:192, 0:192] = kproj[2 * h]
        kp[h, 192:384, 192:384] = kproj[2 * h + 1]

    rows16 = lax.broadcasted_iota(jnp.int32, (16, 1), 0)
    crosses = jnp.logical_and(par == 1, unit < UNITS - 1)
    for h in range(2):
        rows = own[h].astype(F32).reshape(4, 16, 640)
        begins = jnp.sum(rows * mix[h, 0:16][None], axis=1)
        ends = jnp.sum(rows * mix[h, 16:32][None], axis=1)
        shares = jnp.concatenate([ends[0:1], ends[1:4] + begins[0:3]], 0)
        placed = jnp.where(rows16 // 4 == member, jnp.concatenate([shares] * 4, 0), 0.0)
        within = jnp.logical_and(rows16 == 4 * (member + 1), par == 0)
        tile[h] = placed + jnp.where(within, begins[3:4], 0.0)
        tail[h] = jnp.where(rows16[0:8] == 0, begins[3:4], 0.0)

    next_row = (row < 63).astype(jnp.int32)
    targets = jnp.where(c == 0, 7, 2 * (3 - x) + 1) + 2 * next_row + jnp.where(row > 0, x + 3, 0)
    pl.semaphore_wait(
        barrier,
        targets + 4 * crosses.astype(jnp.int32) + 10 + (16 - z - par) // 2)

    def quad_copy(m_to, m_from, device):
        return remote(tile.at[m_to // 2], quad.at[m_from], quad_s.at[m_to], quad_r.at[m_from], device)

    for m in range(4):
        @pl.when(m != member)
        def _():
            quad_copy(m, member, (ctx - c + m // 2, x - par + m % 2)).start()

    follower = unit + 1
    run = (follower % 8) // 4

    def tail_copy(h, p):
        device = (2 * (follower // 8) + h, 2 * ((follower % 4) // 2) + p)
        return remote(tail.at[h], tail_in.at[run], tail_s.at[h, p], tail_r.at[run], device)

    def tails(act):
        @pl.when(crosses)
        def _():
            for h in range(2):
                for p in range(2):
                    act(tail_copy(h, p))

    tails(lambda copy: copy.start())

    def win_copy(h, nxt, x_to, slot, device):
        return remote(own.at[h], win.at[h, slot], win_s.at[h, nxt, x_to], win_r.at[slot], device)

    def win_targets(act):
        for nxt in (1, 0):
            for m in range(4 - 3 * nxt):
                x_to = (x + m) % 4
                slot = unit - (8 * (row + nxt) + x_to - 8)
                needed = jnp.logical_and(slot >= 0, slot <= 12)
                needed = jnp.logical_and(needed, row + nxt < 64)
                for h in range(2):
                    ctx_to = 2 * (row + nxt) + h
                    other = jnp.logical_or(ctx_to != ctx, x_to != x)

                    @pl.when(jnp.logical_and(needed, other))
                    def _():
                        act(win_copy(h, nxt, x_to, slot, (ctx_to, x_to)))

    win_targets(lambda copy: copy.start())
    own_copy = pltpu.make_async_copy(own.at[c], win.at[c, 8 + 4 * c], own_sem)
    own_copy.start()

    @pl.when(row == 0)
    def _():
        def clear(s):
            win[c, s] = jnp.zeros((64, 640), BF)

        loop(0, 8 - x, clear)

    def clear_plane(zz):
        @pl.when(zz % 2 == zp)
        def _():
            comp[c, zz // 2, zz % 2, y, half] = jnp.zeros((16, 640), BF)

    loop(z + 1, 4 * (z // 4) + 4, clear_plane)

    @pl.when((z // 4) % 2 == 0)
    def _():
        def clear(i):
            comp[:, 2 * (z // 4) + 2 + i] = jnp.zeros((2, 2, 4, 2, 16, 640), BF)

        loop(0, 2, clear)

    total = tile[c]
    for m in range(4):
        @pl.when(m != member)
        def _():
            quad_copy(m, m, (ctx, x)).wait_recv()
    for k in range(2):
        @pl.when(run_before(k) >= 0)
        def _():
            remote(tail.at[0], tail_in.at[k], tail_s.at[0, 0], tail_r.at[k], sibling).wait_recv()

        @pl.when(run_before(k) < 0)
        def _():
            tail_in[k] = jnp.zeros((8, 640), F32)

    for m in range(4):
        total = total + jnp.where(m == member, 0.0, quad[m])
    total = total + jnp.concatenate([tail_in[0], tail_in[1]], 0)
    pooled = total.astype(BF)
    keys = jnp.dot(pooled[:, 0:384], kp[c], preferred_element_type=F32)
    v0 = jnp.dot(pooled[:, 384:512], vproj[2 * c], preferred_element_type=F32)
    v1 = jnp.dot(pooled[:, 512:640], vproj[2 * c + 1], preferred_element_type=F32)
    no_block = jnp.logical_and(jnp.logical_and(row == 0, half == 0), rows16 == 0)
    piece[:, 0:384] = jnp.where(no_block, keys[1:2], keys).astype(BF)
    piece[:, 384:512] = jnp.where(no_block, 0.0, v0).astype(BF)
    piece[:, 512:640] = jnp.where(no_block, 0.0, v1).astype(BF)

    @pl.when(par == 1)
    def _():
        comp[c, z // 2, z % 2, y, half] = piece[...]

    def z_copy(z_from, z_to):
        ref = comp.at[c, z_from // 2, z_from % 2, y, half]
        return remote(piece, ref, z_s.at[z_to], z_r.at[z_from], (z_to * 8 + y * 2 + c, x))

    later(lambda zz: z_copy(z, zz).start())

    lane = lax.broadcasted_iota(jnp.int32, (64, 256), 1)
    zero = jnp.zeros((64, 256), F32)
    q_copy.wait()
    for head in range(64):
        g, hh = head // 16, head % 16
        at = 384 * (head // 2) + 128 * (head % 2)
        t = q_ref[:, at:at + 256].astype(F32)
        if head % 2 != g % 2:
            t = pltpu.roll(t, 192 if head % 2 else 64, 1)
        t = jnp.where(lane < 192 if g % 2 == 0 else lane >= 64, t, zero)
        qs[g, 64 * hh:64 * hh + 64, :] = t.astype(BF)
    sig = jax.nn.sigmoid(gates[...].astype(F32))
    for head in range(64):
        g, hh = head // 16, head % 16
        gc[g, 64 * hh:64 * hh + 64, :] = jnp.broadcast_to(sig[:, 2 * head:2 * head + 1], (64, 128))
        gw[g, 64 * hh:64 * hh + 64, :] = jnp.broadcast_to(sig[:, 2 * head + 1:2 * head + 2], (64, 128))
    vx[:, :, 128:256] = jnp.ones((4, KC, 128), BF)

    i = lax.broadcasted_iota(jnp.int32, (64, WK), 0)
    k = lax.broadcasted_iota(jnp.int32, (64, WK), 1)
    bw[...] = jnp.where((k > i) & (k <= i + 512) & (k + 64 * (unit - 8) >= 0), 0.0, NEG)
    last_chunk = z // 8
    i = lax.broadcasted_iota(jnp.int32, (64, KC), 0)
    k = lax.broadcasted_iota(jnp.int32, (64, KC), 1)
    r = k % 128
    m = (r % 16) // 4
    u = 8 * (4 * (8 * last_chunk + k // 128) + r // 32) + 4 * (m // 2) + 2 * ((r % 32) // 16) + m % 2
    b = 4 * u - 1 + r % 4
    bc[...] = jnp.where((16 * b + 31 <= 64 * unit + i) & (b >= 0), 0.0, NEG)

    def pass_copy(k, m):
        x_to = (x + m) % 4
        return remote(
            win.at[c, 4 * k], win.at[c, 4 * k + x - x_to], pass_s.at[k, m], win_r.at[4 * k + x - x_to], (ctx, x_to))

    def passes(k, act):
        for m in (1, 3, 2):
            @pl.when(jnp.logical_or(k == 1, (x + m) % 4 < x))
            def _():
                act(pass_copy(k, m))

    def win_wait(s):
        remote(own.at[0], win.at[c, s], win_s.at[0, 0, 0], win_r.at[s], sibling).wait_recv()

    @pl.when(row > 0)
    def _():
        for k in (1, 0):
            win_wait(4 * k)
            passes(k, lambda copy: copy.start())

    await_planes(0, near_planes)

    def peer(along_x, d):
        if along_x:
            return (ctx, (x + d) % 4)
        return (z * 8 + ((y + d) % 4) * 2 + c, x)

    def a_copy(ci, d, xx, yy):
        pp = (z + xx % 2 + 1) % 2
        ref = comp.at[c, pl.ds(2 * ci, 2), pp, yy, xx // 2]
        return remote(ref, ref, a_s.at[ci, d - 1], a_r.at[ci, d - 1], peer(ci % 2 == 0, d))

    def b_copy(ci, d, xx, yy):
        if ci % 2 == 0:
            ref = comp.at[c, pl.ds(2 * ci, 2), :, yy]
        else:
            ref = comp.at[c, pl.ds(2 * ci, 2), (z + xx % 2 + 1) % 2, :, xx // 2]
        return remote(ref, ref, b_s.at[ci, d - 1], b_r.at[ci, d - 1], peer(ci % 2 == 1, d))

    def d_copy(ci, cc):
        ref = comp.at[cc, pl.ds(2 * ci, 2)]
        return remote(ref, ref, d_s.at[ci], d_r.at[ci], sibling)

    def back(along_x, d):
        return ((x + 4 - d) % 4, y) if along_x else (x, (y + 4 - d) % 4)

    def chunks(which, act):
        for ci in which:
            @pl.when(4 * ci <= z)
            def _():
                act(ci)

    def send_a(ci):
        for d in (1, 3, 2):
            a_copy(ci, d, x, y).start()

    def send_b(ci):
        for d in (1, 3, 2):
            a_copy(ci, d, *back(ci % 2 == 0, d)).wait_recv()
        for d in (1, 3, 2):
            b_copy(ci, d, x, y).start()

    def send_d(ci):
        for d in (1, 3, 2):
            b_copy(ci, d, *back(ci % 2 == 1, d)).wait_recv()
        d_copy(ci, c).start()

    @pl.when(z >= 8)
    def _():
        chunks((3, 2), send_a)

    @pl.when(z < 8)
    def _():
        chunks((1, 0), send_a)

    def nearest(act):
        @pl.when(z >= 8)
        def _():
            chunks((3, 2), act)

        @pl.when(z < 8)
        def _():
            chunks((1, 0), act)

    def farther(act):
        @pl.when(z >= 8)
        def _():
            chunks((1, 0), act)

    nearest(send_b)
    await_planes(near_planes, (z + 1 - par) // 2)
    farther(send_a)

    def win_rest(s):
        @pl.when(jnp.logical_and(s != 0, s != 4))
        def _():
            win_wait(s)

    source_slots(win_rest)
    own_copy.wait()

    def relay(cc, first):
        ref = win.at[cc, pl.ds(4 * first, 9)]
        return remote(ref, ref, rel_s, rel_r, sibling)

    relay(c, 1 - c).start()

    def scores(g, tile, keys):
        q = qs[g, pl.ds(pl.multiple_of(tile * RT, RT), RT), :]
        return lax.dot_general(q, keys, (((1,), (1,)), ((), ())), preferred_element_type=F32)

    def biased(s, bias):
        width = s.shape[1]
        return (s.reshape(RT // 64, 64, width) + bias[...][None]).reshape(RT, width)

    def win_keys(h, odd):
        return win[h, pl.ds(4 * c, 9), :, 128 * odd:128 * odd + 256].reshape(WK, 256)

    def win_done(s, g, tile):
        rows = pl.ds(pl.multiple_of(tile * RT, RT), RT)
        s = biased(s, bw)
        top = jnp.max(s, axis=1, keepdims=True)
        p = jnp.exp((s - top) * SCALE).astype(BF)
        a = jnp.dot(p, vx[g, 0:WK, :], preferred_element_type=F32)
        owin[g, rows, :] = gw[g, rows, :] * a[:, 0:128] / a[:, 128:256]

    def comp_keys(h, odd, chunk):
        return comp[h, pl.ds(4 * chunk, 4), :, :, :, :, 128 * odd:128 * odd + 256].reshape(KC, 256)

    def comp_done(s, g, tile, first):
        rows = pl.ds(pl.multiple_of(tile * RT, RT), RT)
        if first:
            s = biased(s, bc)
            top = jnp.maximum(jnp.max(s, axis=1, keepdims=True), FLOOR)
            p = jnp.exp((s - top) * SCALE).astype(BF)
            acc[g, rows, :] = jnp.dot(p, vx[g], preferred_element_type=F32)
        else:
            before = mx[g, rows, 0:1]
            top = jnp.maximum(jnp.max(s, axis=1, keepdims=True), before)
            p = jnp.exp((s - top) * SCALE).astype(BF)
            factor = jnp.exp((before - top) * SCALE)
            acc[g, rows, :] = acc[g, rows, :] * factor + jnp.dot(p, vx[g], preferred_element_type=F32)
        mx[g, rows, :] = jnp.broadcast_to(top, (RT, 128))

    tiles = 1024 // RT

    def run_half(h, width, keys, done):
        s0[:, 0:width] = scores(2 * h, 0, keys(h, 0))

        def body(t):
            s1[:, 0:width] = scores(2 * h + 1, t, keys(h, 1))
            done(s0[:, 0:width], 2 * h, t)
            s0[:, 0:width] = scores(2 * h, jnp.minimum(t + 1, tiles - 1), keys(h, 0))
            done(s1[:, 0:width], 2 * h + 1, t)

        loop(0, tiles, body)

    def win_half(h):
        for odd in range(2):
            at = 384 + 128 * odd
            vx[2 * h + odd, 0:WK, 0:128] = win[h, pl.ds(4 * c, 9), :, at:at + 128].reshape(WK, 128)
        run_half(h, WK, win_keys, win_done)

    def comp_half(h, chunk, first):
        for odd in range(2):
            at = 384 + 128 * odd
            vx[2 * h + odd, :, 0:128] = comp[h, pl.ds(4 * chunk, 4), :, :, :, :, at:at + 128].reshape(KC, 128)
        weight = jnp.where(jnp.logical_and(chunk == 0, rows16 == 0), 0.0, 1.0).astype(BF)
        for odd in range(2):
            vx[2 * h + odd, 0:16, 128:256] = jnp.broadcast_to(weight, (16, 128))
        run_half(h, KC, lambda hh, odd: comp_keys(hh, odd, chunk),
                 lambda s, g, t: comp_done(s, g, t, first))

    def wait_d(ci):
        d_copy(ci, 1 - c).wait_recv()

    win_half(c)
    relay(1 - c, c).wait_recv()
    win_half(1 - c)
    nearest(send_d)
    farther(send_b)
    comp_half(c, last_chunk, True)
    nearest(wait_d)
    comp_half(1 - c, last_chunk, True)
    farther(send_d)

    @pl.when(z >= 8)
    def _():
        comp_half(c, jnp.int32(0), False)

    farther(wait_d)

    @pl.when(z >= 8)
    def _():
        comp_half(1 - c, jnp.int32(0), False)

    for g in range(4):
        for hh in range(16):
            rows = slice(64 * hh, 64 * hh + 64)
            weight = acc[g, rows, 128:256]
            o = gc[g, rows, :] * acc[g, rows, 0:128] / jnp.where(weight > 0.0, weight, 1.0) + owin[g, rows, :]
            at = 128 * (16 * g + hh)
            out[:, at:at + 128] = o.astype(BF)

    def sent(ci):
        d_copy(ci, c).wait_send()
        for d in (1, 2, 3):
            a_copy(ci, d, x, y).wait_send()
            b_copy(ci, d, x, y).wait_send()

    chunks((3, 2, 1, 0), sent)
    relay(c, 1 - c).wait_send()
    win_targets(lambda copy: copy.wait_send())

    @pl.when(row > 0)
    def _():
        for k in (1, 0):
            passes(k, lambda copy: copy.wait_send())

    later(lambda zz: z_copy(z, zz).wait_send())
    for m in range(4):
        @pl.when(m != member)
        def _():
            quad_copy(m, member, (ctx, x)).wait_send()

    tails(lambda copy: copy.wait_send())


def local(queries, key_rows, values, gate_logits, key_mix, key_proj, value_mix, value_proj):
    dma = pltpu.SemaphoreType.DMA
    vmem = pl.BlockSpec(memory_space=pltpu.VMEM)
    return pl.pallas_call(
        fused_kernel,
        out_shape=jax.ShapeDtypeStruct((64, 8192), BF),
        in_specs=[pl.BlockSpec(memory_space=pl.ANY)] + [vmem] * 7,
        out_specs=vmem,
        scratch_shapes=[
            pltpu.VMEM((64, 12288), BF),
            pltpu.VMEM((2, 64, 640), BF),
            pltpu.VMEM((2, 32, 640), F32),
            pltpu.VMEM((2, 384, 384), BF),
            pltpu.VMEM((2, 16, 640), F32),
            pltpu.VMEM((2, 8, 640), F32),
            pltpu.VMEM((4, 16, 640), F32),
            pltpu.VMEM((2, 8, 640), F32),
            pltpu.VMEM((16, 640), BF),
            pltpu.VMEM((2, 13, 64, 640), BF),
            pltpu.VMEM((2, 8, 2, 4, 2, 16, 640), BF),
            pltpu.VMEM((4, 1024, 256), BF),
            pltpu.VMEM((4, 1024, 128), F32),
            pltpu.VMEM((4, 1024, 128), F32),
            pltpu.VMEM((4, KC, 256), BF),
            pltpu.VMEM((4, 1024, 256), F32),
            pltpu.VMEM((4, 1024, 128), F32),
            pltpu.VMEM((4, 1024, 128), F32),
            pltpu.VMEM((RT, KC), F32),
            pltpu.VMEM((RT, KC), F32),
            pltpu.VMEM((64, WK), F32),
            pltpu.VMEM((64, KC), F32),
            dma, dma((2, 2)), dma((2,)), dma((2, 2, 4)), dma((13,)), dma, dma, dma, dma((4,)), dma((4,)), dma((16,)), dma((16,)),
            dma((4, 3)), dma((4, 3)), dma((4, 3)), dma((4, 3)), dma((4,)), dma((4,)), dma((2, 4)),
        ],
        compiler_params=pltpu.CompilerParams(
            collective_id=0, has_side_effects=True, vmem_limit_bytes=56 * 2**20),
        cost_estimate=pl.CostEstimate(flops=10**10, bytes_accessed=10**7, transcendentals=10**7),
    )(queries, key_rows, values, gate_logits, key_mix, key_proj, value_mix, value_proj)


def solution(mesh):
    rows = P(("ctx", "head"), None)
    return jax.shard_map(
        local, mesh=mesh, in_specs=(rows,) * 4 + (P(),) * 4, out_specs=rows, check_vma=False)
```
